32 devices in a mesh: seq: 8 (over z, y), pb: 4 (over x, core).
Axes of the slice: x: 2, y: 2, z: 4, core: 2. Of those that a mesh axis runs over, the one named last changes fastest.
Arguments:
- tokens: bfloat16 [2048, 2048], P('seq'), may hold values from -0.119628906 to 0.119628906
- w_query: bfloat16 [2048, 2048], P(None, 'pb')
- w_key: bfloat16 [2048, 2048], P(None, 'pb')
- w_value: bfloat16 [2048, 2048], P(None, 'pb'), may hold values from -0.125 to 0.125
- w_out: bfloat16 [2048, 2048], P('pb'), may hold values from -0.125 to 0.125
- gain_attn: float32 [2048], replicated, may hold values from 0.1 to 1.9
- gain_embed: float32 [2048], replicated, may hold values from 0.1 to 1.9
- queries: bfloat16 [32, 32, 2048], P(('seq', 'pb')), may hold values from -0.125 to 0.125
- query_lengths: int32 [32], P(('seq', 'pb')), may hold values from 8 to 32
- group_lengths: int32 [16], replicated, may hold values from 1 to 1024, 2048 in all
- teacher: float32 [32, 16], P(('seq', 'pb')), may hold values from -12 to 12
Outputs:
- embedded: bfloat16 [2048, 2048], P('seq')
- scores: float32 [32, 16], P(('seq', 'pb'))
- score_gradient: float32 [32, 16], P(('seq', 'pb'))
- distill_loss: float32 [], replicated
The draws below stay inside these ranges and needn't reach their ends.
Inputs may be any that keep to these rules, and one draw needn't show every extreme that they name: `group_lengths`: the groups cover the document in order: the lengths sum to 2048.
All inputs are finite; a program needn't handle non-finite values.
Results may differ from the reference program's by a relative error of at most 0.013.
Values may be sent and summed in bfloat16 or wider, within the bound.
A program may use at most 128 MiB of HBM per device.

```python
import math
import jax
import jax.numpy as jnp
import numpy as np
from jax import lax

D = 2048
HEADS = 16
HD = 128
WIN = 2048
LQ = 32
TOK_DEV = 256
TOKENS = 2048
QUERY_COUNT = 32
NCH = 16


def projection_base(key, salt_value):
    return jax.random.normal(jax.random.fold_in(key, salt_value), (D, D), jnp.float32) * D ** (-0.5)


def draw_w_query(key, part):
    return projection_base(key, 101).astype(jnp.bfloat16)


def draw_w_key(key, part):
    drawn = projection_base(key, 202)
    return drawn.astype(jnp.bfloat16)


def set_ends(result, key, smallest, largest):
    index_at = [jax.random.randint(jax.random.fold_in(key, axis), (), 0, length) for axis, length in enumerate(result.shape)]
    main_axis = result.shape.index(max(result.shape))
    next_to = index_at[:main_axis] + [(index_at[main_axis] + 1) % result.shape[main_axis]] + index_at[main_axis + 1:]
    return result.at[tuple(index_at)].set(smallest).at[tuple(next_to)].set(largest)


def shard_levels(stream_key, dims, shards, low, high):
    level = 1.0
    for position, blocks in shards:
        steps = jax.random.uniform(jax.random.fold_in(jax.random.fold_in(stream_key, 6), position), (blocks,), jnp.float32, low / len(shards), high / len(shards))
        level = level * jnp.repeat(jnp.exp(steps), dims[position] // blocks).reshape((-1,) + (1,) * (len(dims) - 1 - position))
    return level


def length_profile(amount, total, reach, lean):
    loads = [(1 << 20) // math.isqrt(grade ** lean) + 1 for grade in range(2, amount + 1)]
    rest, counts = total - reach - (amount - 1), [1] * (amount - 1)
    while rest > 0:
        movable = [i for i in range(amount - 1) if counts[i] < reach]
        mass, left = sum([loads[i] for i in movable]), rest
        for i in movable:
            extra = min(reach - counts[i], max(1, left * loads[i] // mass), rest)
            counts[i] = counts[i] + extra
            rest = rest - extra
    return np.array([reach] + counts)


def ragged(key, amount, total, most, lean):
    if amount == 2:
        one = jax.random.randint(key, (), max(1, total - most), min(most, total - 1) + 1)
        return jnp.stack([one, total - one])
    sizes = jnp.asarray(length_profile(amount, total, most, lean), jnp.int32)
    couples = (amount - 1) // 2
    source_of, receiver = sizes[1:1 + 2 * couples:2], sizes[2:2 + 2 * couples:2]
    room = jnp.minimum(source_of - 1, most - receiver)
    moved = jax.random.randint(jax.random.fold_in(key, 1), (couples,), 0, 1 << 20) % (room + 1)
    sizes = sizes.at[1:1 + 2 * couples:2].set(source_of - moved).at[2:2 + 2 * couples:2].set(receiver + moved)
    return sizes[jax.random.permutation(jax.random.fold_in(key, 2), amount)]


def noise(stream_key, dims, width, reach, shards=(), kind=jnp.bfloat16):
    factor_of = shard_levels(stream_key, dims, shards, -0.22, 0.18) if shards else 1.0
    values = jax.random.normal(stream_key, dims, jnp.float32) * width * factor_of
    return jnp.minimum(jnp.maximum(values, -reach), reach).astype(kind)


def setup_inputs(seed: int = 0) -> dict:
    arg_keys = jax.random.split(jax.random.key(seed), 12)
    tokens = noise(arg_keys[0], (TOKENS, D), 0.02, 0.119628906, ((0, 8),))
    w_query = draw_w_query(jax.random.fold_in(arg_keys[11], 71), 0)
    w_key = draw_w_key(jax.random.fold_in(arg_keys[11], 71), 0)
    w_value = noise(arg_keys[3], (D, D), D ** -0.5, 0.125, ((1, 4),))
    w_out = noise(arg_keys[4], (D, D), D ** -0.5, 0.125, ((0, 4),))
    gain_attn = jnp.clip(1.0 + 0.18 * jax.random.normal(arg_keys[5], (D,), jnp.float32), 0.1, 1.9)
    gain_embed = jnp.clip(1.0 + 0.18 * jax.random.normal(arg_keys[6], (D,), jnp.float32), 0.1, 1.9)
    queries = noise(arg_keys[7], (QUERY_COUNT, LQ, D), D ** -0.5, 0.125, ((0, 32),))
    query_lengths = set_ends(jax.random.randint(arg_keys[8], (QUERY_COUNT,), LQ // 4, LQ + 1), jax.random.fold_in(arg_keys[8], 1), LQ // 4, LQ).astype(jnp.int32)
    group_lengths = ragged(arg_keys[9], NCH, TOKENS, 4 * TOK_DEV, 2).astype(jnp.int32)
    teacher = noise(arg_keys[10], (QUERY_COUNT, NCH), 3.0, 12.0, ((0, 32),), jnp.float32)
    return dict(tokens=tokens, w_query=w_query, w_key=w_key, w_value=w_value, w_out=w_out, gain_attn=gain_attn, gain_embed=gain_embed, queries=queries, query_lengths=query_lengths, group_lengths=group_lengths, teacher=teacher)


EPSILON = 1e-06
SOFTMAX_TEMP = 0.1

def rms_scale(values, gain):
    mean_sq = lax.optimization_barrier(jnp.mean(values * values, axis=-1, keepdims=True))
    return values * lax.rsqrt(mean_sq + EPSILON) * gain

def segmented_max(values, group_id):
    span_len = values.shape[-1]
    stride = 1
    while stride < span_len:
        filler = jnp.full(values.shape[:-1] + (stride,), -jnp.inf, values.dtype)
        shifted = jnp.concatenate([filler, values[..., :-stride]], axis=-1)
        prior_id = jnp.concatenate([jnp.full((stride,), -1, jnp.int32), group_id[:-stride]])
        values = jnp.where((prior_id == group_id)[None, :], jnp.maximum(values, shifted), values)
        stride = stride * 2
    return values

def reference(tokens, w_query, w_key, w_value, w_out, gain_attn, gain_embed, queries, query_lengths, group_lengths, teacher):
    half_win = WIN // 2
    residual = tokens.astype(jnp.float32)
    normed = rms_scale(residual, gain_attn).astype(jnp.bfloat16)
    q_all = jnp.dot(normed, w_query, preferred_element_type=jnp.float32).astype(jnp.bfloat16)
    k_all = jnp.dot(normed, w_key, preferred_element_type=jnp.float32).astype(jnp.bfloat16)
    v_all = jnp.dot(normed, w_value, preferred_element_type=jnp.float32).astype(jnp.bfloat16)
    k_pad = jnp.pad(k_all, ((half_win, half_win), (0, 0)))
    v_pad = jnp.pad(v_all, ((half_win, half_win), (0, 0)))
    block_rows = math.gcd(512, TOKENS)
    span_rows = block_rows + 2 * half_win

    def attend(block_index):
        first_row = (block_index * block_rows).astype(jnp.int32)
        q_block = lax.dynamic_slice_in_dim(q_all, first_row, block_rows, 0).reshape(block_rows, HEADS, HD).astype(jnp.float32)
        k_block = lax.dynamic_slice_in_dim(k_pad, first_row, span_rows, 0).reshape(span_rows, HEADS, HD).astype(jnp.float32)
        v_block = lax.dynamic_slice_in_dim(v_pad, first_row, span_rows, 0).reshape(span_rows, HEADS, HD).astype(jnp.float32)
        logits = jnp.einsum('qhd,khd->hqk', q_block, k_block) * HD ** (-0.5)
        q_pos = first_row + jnp.arange(block_rows, dtype=jnp.int32)
        k_pos = first_row - half_win + jnp.arange(span_rows, dtype=jnp.int32)
        in_window = (jnp.abs(q_pos[:, None] - k_pos[None, :]) <= half_win) & (k_pos >= 0)[None, :] & (k_pos < TOKENS)[None, :]
        logits = jnp.where(in_window[None], logits, -jnp.inf)
        row_max = lax.optimization_barrier(jnp.max(logits, axis=-1, keepdims=True))
        exp_terms = jnp.exp(logits - row_max)
        weights = (exp_terms / lax.optimization_barrier(jnp.sum(exp_terms, axis=-1, keepdims=True))).astype(jnp.bfloat16)
        mixed = jnp.einsum('hqk,khd->qhd', weights.astype(jnp.float32), v_block)
        return mixed.reshape(block_rows, HEADS * HD).astype(jnp.bfloat16)
    heads_out = lax.map(attend, jnp.arange(TOKENS // block_rows, dtype=jnp.int32)).reshape(TOKENS, HEADS * HD)
    attn_sum = jnp.dot(heads_out, w_out, preferred_element_type=jnp.float32)
    embedded = rms_scale(residual + attn_sum, gain_embed).astype(jnp.bfloat16)
    group_end = jnp.cumsum(group_lengths).astype(jnp.int32)
    positions = jnp.arange(TOKENS, dtype=jnp.int32)
    group_id = lax.optimization_barrier(jnp.sum((group_end[None, :] <= positions[:, None]).astype(jnp.int32), axis=1)).astype(jnp.int32)
    last_token = (group_end - 1).astype(jnp.int32)

    def score_one(query_item):
        q_tok, length = query_item
        similar = jnp.dot(q_tok, embedded.T, preferred_element_type=jnp.float32)
        running = segmented_max(similar, group_id)
        picked = jnp.take(running, last_token, axis=1)
        live_mask = (jnp.arange(LQ, dtype=jnp.int32) < length).astype(jnp.float32)
        return lax.optimization_barrier(jnp.sum(picked * live_mask[:, None], axis=0)) / length.astype(jnp.float32)
    scores = lax.map(score_one, (queries, query_lengths))
    student_scores = scores / SOFTMAX_TEMP
    student_scores = student_scores - lax.optimization_barrier(jnp.max(student_scores, axis=-1, keepdims=True))
    student_log_prob = student_scores - jnp.log(lax.optimization_barrier(jnp.sum(jnp.exp(student_scores), axis=-1, keepdims=True)))
    target_scores = teacher / SOFTMAX_TEMP
    target_scores = target_scores - lax.optimization_barrier(jnp.max(target_scores, axis=-1, keepdims=True))
    log_t = target_scores - jnp.log(lax.optimization_barrier(jnp.sum(jnp.exp(target_scores), axis=-1, keepdims=True)))
    teacher_prob = jnp.exp(log_t)
    kl_terms = lax.optimization_barrier(jnp.sum(teacher_prob * (log_t - student_log_prob), axis=-1))
    distill_loss = jnp.sum(kl_terms) / QUERY_COUNT
    score_gradient = (jnp.exp(student_log_prob) - teacher_prob) / (SOFTMAX_TEMP * QUERY_COUNT)
    return (embedded, scores, score_gradient, distill_loss)
```

```python
import functools

import jax
import jax.numpy as jnp
from jax import lax
from jax.experimental import pallas as pl
from jax.experimental.pallas import tpu as pltpu
from jax.sharding import PartitionSpec as P

HD = 128
HEADS = 16
WIN = 2048
LQ = 32


EPSILON = 1e-06
SOFTMAX_TEMP = 0.1


def shifted_2(x, axis, by):
    count = lax.axis_size(axis)
    pairs = [(i, i + by) for i in range(count) if 0 <= i + by < count]
    return lax.ppermute(x, axis, pairs)


def rms_scale(values, gain):
    mean_sq = jnp.mean(values * values, axis=-1, keepdims=True)
    return values * lax.rsqrt(mean_sq + EPSILON) * gain


def segmented_max(values, group_id):
    span_len = values.shape[-1]
    stride = 1
    while stride < span_len:
        filler = jnp.full(values.shape[:-1] + (stride,), -jnp.inf, values.dtype)
        shifted = jnp.concatenate([filler, values[..., :-stride]], axis=-1)
        prior_id = jnp.concatenate([jnp.full((stride,), -1, jnp.int32), group_id[:-stride]])
        values = jnp.where((prior_id == group_id)[None, :], jnp.maximum(values, shifted), values)
        stride = stride * 2
    return values


def per_device(
    tokens,
    w_query,
    w_key,
    w_value,
    w_out,
    gain_attn,
    gain_embed,
    queries,
    query_lengths,
    group_lengths,
    teacher,
):
    shard_rows = tokens.shape[0]
    seq_count = lax.axis_size("seq")
    seq_place = lax.axis_index("seq")
    head_width = w_query.shape[1]
    heads_here = head_width // HD
    half_win = WIN // 2
    reach_count = half_win // shard_rows
    my_start = seq_place * shard_rows
    total_tokens = shard_rows * seq_count
    residual = tokens.astype(jnp.float32)
    normed = rms_scale(residual, gain_attn).astype(jnp.bfloat16)
    q_local = jnp.dot(normed, w_query, preferred_element_type=jnp.float32).astype(jnp.bfloat16)
    k_local = jnp.dot(normed, w_key, preferred_element_type=jnp.float32).astype(jnp.bfloat16)
    v_local = jnp.dot(normed, w_value, preferred_element_type=jnp.float32).astype(jnp.bfloat16)
    key_value = jnp.stack([k_local, v_local])
    earlier = [shifted_2(key_value, "seq", distance) for distance in range(reach_count, 0, -1)]
    later = [shifted_2(key_value, "seq", -distance) for distance in range(1, reach_count + 1)]
    window = jnp.concatenate(earlier + [key_value] + later, axis=1)
    span_rows = window.shape[1]
    q_pos = my_start + jnp.arange(shard_rows, dtype=jnp.int32)
    k_pos = my_start - reach_count * shard_rows + jnp.arange(span_rows, dtype=jnp.int32)
    in_window = (
        (jnp.abs(q_pos[:, None] - k_pos[None, :]) <= half_win)
        & (k_pos >= 0)[None, :]
        & (k_pos < total_tokens)[None, :]
    )
    q_heads = q_local.reshape(shard_rows, heads_here, HD)
    k_heads = window[0].reshape(span_rows, heads_here, HD)
    v_heads = window[1].reshape(span_rows, heads_here, HD)
    logits = jnp.einsum(
        "qhd,khd->hqk", q_heads, k_heads, preferred_element_type=jnp.float32
    ) * HD ** (-0.5)
    logits = jnp.where(in_window[None], logits, -jnp.inf)
    row_max = jnp.max(logits, axis=-1, keepdims=True)
    exp_terms = jnp.exp(logits - row_max)
    weights = (exp_terms / jnp.sum(exp_terms, axis=-1, keepdims=True)).astype(jnp.bfloat16)
    mixed = jnp.einsum("hqk,khd->qhd", weights, v_heads, preferred_element_type=jnp.float32)
    mixed = mixed.reshape(shard_rows, head_width).astype(jnp.bfloat16)
    partial_value = jnp.dot(mixed, w_out, preferred_element_type=jnp.float32)
    attn_sum = lax.psum(partial_value, "pb")
    embedded = rms_scale(residual + attn_sum, gain_embed).astype(jnp.bfloat16)
    group_end = jnp.cumsum(group_lengths)
    group_start = group_end - group_lengths
    group_id = jnp.sum((group_end[None, :] <= q_pos[:, None]).astype(jnp.int32), axis=1)
    last_local = jnp.clip(group_end - 1 - my_start, 0, shard_rows - 1)
    present = (group_start < my_start + shard_rows) & (group_end > my_start)
    q_piece = lax.all_gather(queries, "seq", axis=0, tiled=True)
    count = q_piece.shape[0]
    q_rows = q_piece.reshape(count * q_piece.shape[1], q_piece.shape[2])
    similar = jnp.einsum("td,rd->tr", q_rows, embedded, preferred_element_type=jnp.float32)
    running = segmented_max(similar, group_id)
    picked = jnp.take(running, last_local, axis=1)
    picked = jnp.where(present[None, :], picked, -jnp.inf)
    part_max = picked.reshape(count, q_piece.shape[1], picked.shape[-1])
    own_count = queries.shape[0]
    all_maxima = lax.pmax(part_max, "seq")
    token_max = lax.dynamic_slice_in_dim(all_maxima, seq_place * own_count, own_count, 0)
    live_mask = (jnp.arange(LQ, dtype=jnp.int32)[None, :] < query_lengths[:, None]).astype(
        jnp.float32
    )
    scores = (
        jnp.sum(token_max * live_mask[:, :, None], axis=1)
        / query_lengths.astype(jnp.float32)[:, None]
    )
    student_scores = scores / SOFTMAX_TEMP
    student_scores = student_scores - jnp.max(student_scores, axis=-1, keepdims=True)
    student_log_prob = student_scores - jnp.log(
        jnp.sum(jnp.exp(student_scores), axis=-1, keepdims=True)
    )
    target_scores = teacher / SOFTMAX_TEMP
    target_scores = target_scores - jnp.max(target_scores, axis=-1, keepdims=True)
    log_t = target_scores - jnp.log(jnp.sum(jnp.exp(target_scores), axis=-1, keepdims=True))
    teacher_prob = jnp.exp(log_t)
    kl_terms = jnp.sum(teacher_prob * (log_t - student_log_prob), axis=-1)
    query_count_all = own_count * seq_count * lax.axis_size("pb")
    distill_loss = lax.psum(jnp.sum(kl_terms), ("seq", "pb")) / query_count_all
    score_gradient = (jnp.exp(student_log_prob) - teacher_prob) / (SOFTMAX_TEMP * query_count_all)
    return (embedded, scores, score_gradient, distill_loss)


MESH = pl.DeviceIdType.MESH
NEG = float("-inf")


def fused_kernel(
    seq_count,
    pb_count,
    lengths_ref,
    groups_ref,
    tokens_ref,
    gain_attn_ref,
    gain_embed_ref,
    queries_ref,
    teacher_ref,
    wk_hbm,
    wv_hbm,
    wq_hbm,
    wo_hbm,
    emb_hbm,
    scores_ref,
    grad_ref,
    loss_ref,
    wk,
    wv,
    wq,
    wo,
    kv_send,
    q_send,
    kv,
    q_in,
    m_send,
    m_in,
    query_all,
    a_send,
    a_in,
    own_sum,
    b_send,
    b_in,
    emb,
    sim,
    gmax,
    kl_seq,
    kl_pb,
    w_sem,
    out_sem,
    send,
    recv,
):
    me = lax.axis_index("seq")
    pb = lax.axis_index("pb")
    planes = seq_count // 2
    z, y = me // 2, lax.rem(me, 2)
    core = lax.rem(pb, 2)
    core_mate = pb + 1 - 2 * core
    x_mate = lax.rem(pb + 2, pb_count)
    y_mate = me + 1 - 2 * y
    rows = tokens_ref.shape[0]
    half = rows // 2
    chunk = half // 2
    own_rows = pl.multiple_of(core * half, half)
    mate_rows = pl.multiple_of((1 - core) * half, half)
    groups = groups_ref.shape[0]

    QZ, QY, KZ, KY, TQ = 0, planes, 2 * planes, 3 * planes, 4 * planes
    MX, CA, CB, CD = 5 * planes, 6 * planes, 6 * planes + 1, 6 * planes + 3
    GM = 6 * planes + 5
    LS, LP = GM + seq_count, GM + 2 * seq_count

    def remote(src, dst, out_place, in_place, where):
        return pltpu.make_async_remote_copy(
            src_ref=src,
            dst_ref=dst,
            send_sem=send.at[out_place],
            recv_sem=recv.at[in_place],
            device_id=where,
            device_id_type=MESH,
        )

    loads = [
        pltpu.make_async_copy(src, dst, w_sem.at[i])
        for i, (src, dst) in enumerate(((wk_hbm, wk), (wv_hbm, wv), (wq_hbm, wq), (wo_hbm, wo)))
    ]
    for load in loads:
        load.start()

    barrier = pltpu.get_barrier_semaphore()
    for d in range(1, seq_count):
        pl.semaphore_signal(
            barrier,
            inc=1,
            device_id={"seq": lax.rem(me + d, seq_count)},
            device_id_type=MESH,
        )
    for d in range(1, pb_count):
        pl.semaphore_signal(
            barrier,
            inc=1,
            device_id={"pb": lax.rem(pb + d, pb_count)},
            device_id_type=MESH,
        )
    query_all[me] = queries_ref[0]
    residual = tokens_ref[...].astype(jnp.float32)
    normed = rms_scale(residual, gain_attn_ref[...]).astype(jnp.bfloat16)
    pl.semaphore_wait(barrier, seq_count + pb_count - 2)

    def along(d):
        return lax.rem(z + d, planes)

    sent = []

    def go(copy):
        copy.start()
        sent.append(copy)

    for d in range(1, planes):
        other = along(d)
        go(remote(query_all.at[me], query_all.at[me], QZ + other, QZ + z, {"seq": 2 * other + y}))

    loads[0].wait()
    k_all = jnp.dot(normed, wk[...], preferred_element_type=jnp.float32).astype(jnp.bfloat16)
    for h in range(planes):
        kv_send[h, 0] = k_all[:, h * HD : (h + 1) * HD]
    loads[1].wait()
    v_all = jnp.dot(normed, wv[...], preferred_element_type=jnp.float32).astype(jnp.bfloat16)
    for h in range(planes):
        kv_send[h, 1] = v_all[:, h * HD : (h + 1) * HD]
    for d in range(1, planes):
        other = along(d)
        go(remote(kv_send.at[other], kv.at[me], KZ + other, KZ + z, {"seq": 2 * other + y}))
    kv[me] = kv_send[z]
    go(remote(kv.at[me], kv.at[me], KY + z, KY + z, {"seq": y_mate}))
    loads[2].wait()
    q_all = jnp.dot(normed, wq[...], preferred_element_type=jnp.float32).astype(jnp.bfloat16)
    for h in range(planes):
        q_send[h] = q_all[:, h * HD : (h + 1) * HD]
    for d in range(1, planes):
        other = along(d)
        go(remote(q_send.at[other], q_in.at[z], TQ + other, TQ + z, {"seq": 2 * other + y}))
    q_in[z] = q_send[z]

    for d in range(1, planes):
        source = along(planes - d)
        slot = 2 * source + y
        remote(kv.at[slot], kv.at[slot], KZ + source, KZ + source, {"seq": slot}).wait_recv()
        go(remote(kv.at[slot], kv.at[slot], KY + source, KY + source, {"seq": y_mate}))
    go(remote(query_all.at[me], query_all.at[me], QY + z, QY + z, {"seq": y_mate}))
    for d in range(1, planes):
        source = along(planes - d)
        slot = 2 * source + y
        remote(query_all.at[slot], query_all.at[slot], QZ + source, QZ + source, {"seq": slot}).wait_recv()
        go(remote(query_all.at[slot], query_all.at[slot], QY + source, QY + source, {"seq": y_mate}))
    for d in range(planes):
        source = along(planes - d)
        slot = 2 * source + 1 - y
        remote(kv.at[slot], kv.at[slot], KY + source, KY + source, {"seq": y_mate}).wait_recv()

    span = rows * seq_count
    gap = lax.broadcasted_iota(jnp.int32, (rows, span), 0) - lax.broadcasted_iota(
        jnp.int32, (rows, span), 1
    )

    def attend(source):
        base = (2 * source + y) * rows
        keys = kv[:, 0].reshape(span, HD)
        values = kv[:, 1].reshape(span, HD)
        logits = lax.dot_general(
            q_in[source], keys, (((1,), (1,)), ((), ())), preferred_element_type=jnp.float32
        )
        logits = jnp.where(jnp.abs(gap + base) <= WIN // 2, logits, NEG)
        row_max = jnp.max(logits, axis=-1, keepdims=True)
        terms = jnp.exp((logits - row_max) * HD ** (-0.5))
        total = jnp.sum(terms, axis=-1, keepdims=True)
        out = jnp.dot(terms.astype(jnp.bfloat16), values, preferred_element_type=jnp.float32)
        return (out / total).astype(jnp.bfloat16)

    def block(d, carry):
        source = lax.rem(z + d, planes)
        slot = 2 * source + y
        remote(q_in.at[source], q_in.at[source], TQ + source, TQ + source, {"seq": slot}).wait_recv()
        m_send[source] = attend(source)
        remote(m_send.at[source], m_in.at[z], MX + source, MX + z, {"seq": slot}).start()
        return carry

    lax.fori_loop(1, planes, block, 0)
    m_in[z] = attend(z)
    for d in range(1, planes):
        source = along(planes - d)
        remote(m_in.at[source], m_in.at[source], MX + source, MX + source, {"seq": 2 * source + y}).wait_recv()

    loads[3].wait()

    def project(first):
        mixed = jnp.concatenate([m_in[h, pl.ds(first, half), :] for h in range(planes)], axis=1)
        return jnp.dot(mixed, wo[...], preferred_element_type=jnp.float32)

    a_send[...] = project(mate_rows).astype(jnp.bfloat16)
    copy_a = remote(a_send, a_in, CA, CA, {"pb": core_mate})
    go(copy_a)
    own_sum[...] = project(own_rows)
    copy_a.wait_recv()
    copies_b = []
    for i in range(2):
        part = slice(i * chunk, (i + 1) * chunk)
        b_send[i] = (own_sum[part] + a_in[part].astype(jnp.float32)).astype(jnp.bfloat16)
        copy_b = remote(b_send.at[i], b_in.at[i], CB + i, CB + i, {"pb": x_mate})
        go(copy_b)
        copies_b.append(copy_b)
    for d in range(planes):
        source = along(planes - d)
        slot = 2 * source + 1 - y
        remote(query_all.at[slot], query_all.at[slot], QY + source, QY + source, {"seq": y_mate}).wait_recv()
    for i in range(2):
        here = pl.ds(pl.multiple_of(own_rows + i * chunk, chunk), chunk)
        copies_b[i].wait_recv()
        attn = b_send[i].astype(jnp.float32) + b_in[i].astype(jnp.float32)
        total = tokens_ref[here, :].astype(jnp.float32) + attn
        emb[here, :] = rms_scale(total, gain_embed_ref[...]).astype(jnp.bfloat16)
        go(remote(emb.at[here, :], emb.at[here, :], CD + i, CD + i, {"pb": core_mate}))

    q_rows = query_all[...].reshape(query_all.shape[0] * query_all.shape[1], query_all.shape[2])

    def compare(first):
        sim[pl.ds(first, half), :] = lax.dot_general(
            emb[pl.ds(first, half), :], q_rows, (((1,), (1,)), ((), ())), preferred_element_type=jnp.float32
        )

    compare(own_rows)
    for i in range(2):
        there = pl.ds(pl.multiple_of(mate_rows + i * chunk, chunk), chunk)
        remote(emb.at[there, :], emb.at[there, :], CD + i, CD + i, {"pb": core_mate}).wait_recv()
    store = pltpu.make_async_copy(emb, emb_hbm, out_sem)
    store.start()
    compare(mate_rows)

    similar = sim[...]
    position = lax.broadcasted_iota(jnp.int32, similar.shape, 0) + me * rows
    begin = jnp.int32(0)
    for c in range(groups):
        end = begin + groups_ref[c]
        inside = (position >= begin) & (position < end)
        gmax[me, c : c + 1] = jnp.max(jnp.where(inside, similar, NEG), axis=0, keepdims=True)
        begin = end
    for d in range(1, seq_count):
        other = lax.rem(me + d, seq_count)
        go(remote(gmax.at[me], gmax.at[me], GM + other, GM + me, {"seq": other}))
    for d in range(1, seq_count):
        other = lax.rem(me + d, seq_count)
        remote(gmax.at[other], gmax.at[other], GM + other, GM + other, {"seq": other}).wait_recv()
    token_max = jnp.max(gmax[...], axis=0)
    slot_of = lax.broadcasted_iota(jnp.int32, token_max.shape, 1) - me * LQ
    length = lengths_ref[0]
    live = (slot_of >= 0) & (slot_of < length)
    column = jnp.sum(jnp.where(live, token_max, 0.0), axis=1, keepdims=True)
    square = (groups, groups)
    diagonal = lax.broadcasted_iota(jnp.int32, square, 0) == lax.broadcasted_iota(jnp.int32, square, 1)
    row = jnp.sum(jnp.where(diagonal, column, 0.0), axis=0, keepdims=True)
    scores = row / length.astype(jnp.float32)
    scores_ref[...] = scores

    def log_softmax(values):
        values = values / SOFTMAX_TEMP
        values = values - jnp.max(values, axis=-1, keepdims=True)
        return values - jnp.log(jnp.sum(jnp.exp(values), axis=-1, keepdims=True))

    log_s = log_softmax(scores)
    log_t = log_softmax(teacher_ref[...])
    prob = jnp.exp(log_t)
    amount = seq_count * pb_count
    grad_ref[...] = (jnp.exp(log_s) - prob) / (SOFTMAX_TEMP * amount)
    kl = jnp.sum(prob * (log_t - log_s), axis=-1, keepdims=True)
    kl_seq[me] = jnp.broadcast_to(kl, kl_seq.shape[1:])
    for d in range(1, seq_count):
        other = lax.rem(me + d, seq_count)
        go(remote(kl_seq.at[me], kl_seq.at[me], LS + other, LS + me, {"seq": other}))
    for d in range(1, seq_count):
        other = lax.rem(me + d, seq_count)
        remote(kl_seq.at[other], kl_seq.at[other], LS + other, LS + other, {"seq": other}).wait_recv()
    kl_pb[pb] = jnp.sum(kl_seq[...], axis=0)
    for d in range(1, pb_count):
        other = lax.rem(pb + d, pb_count)
        go(remote(kl_pb.at[pb], kl_pb.at[pb], LP + other, LP + pb, {"pb": other}))
    for d in range(1, pb_count):
        other = lax.rem(pb + d, pb_count)
        remote(kl_pb.at[other], kl_pb.at[other], LP + other, LP + other, {"pb": other}).wait_recv()
    loss_ref[...] = jnp.sum(kl_pb[...], axis=0)[:1, :1] / amount

    for copy in sent:
        copy.wait_send()
    for d in range(1, planes):
        other = along(d)
        remote(m_send.at[other], m_in.at[z], MX + other, MX + z, {"seq": 2 * other + y}).wait_send()
    store.wait()


def fused(
    tokens,
    w_query,
    w_key,
    w_value,
    w_out,
    gain_attn,
    gain_embed,
    queries,
    query_lengths,
    group_lengths,
    teacher,
):
    seq_count, pb_count = lax.axis_size("seq"), lax.axis_size("pb")
    rows, width = tokens.shape
    head_width = w_query.shape[1]
    planes = seq_count // 2
    groups = group_lengths.shape[0]
    slots = queries.shape[0] * seq_count * LQ
    half = rows // 2
    bf, f32 = jnp.bfloat16, jnp.float32
    vmem, smem = pl.BlockSpec(memory_space=pltpu.VMEM), pl.BlockSpec(memory_space=pltpu.SMEM)
    hbm = pl.BlockSpec(memory_space=pl.ANY)
    copies = 6 * planes + 5 + 2 * seq_count + pb_count
    embedded, scores, grad, loss = pl.pallas_call(
        functools.partial(fused_kernel, seq_count, pb_count),
        out_shape=(
            jax.ShapeDtypeStruct((rows, width), bf),
            jax.ShapeDtypeStruct((1, groups), f32),
            jax.ShapeDtypeStruct((1, groups), f32),
            jax.ShapeDtypeStruct((1, 1), f32),
        ),
        in_specs=[smem, smem] + [vmem] * 5 + [hbm] * 4,
        out_specs=(hbm, vmem, vmem, vmem),
        scratch_shapes=[
            pltpu.VMEM((width, head_width), bf),
            pltpu.VMEM((width, head_width), bf),
            pltpu.VMEM((width, head_width), bf),
            pltpu.VMEM((head_width, width), bf),
            pltpu.VMEM((planes, 2, rows, HD), bf),
            pltpu.VMEM((planes, rows, HD), bf),
            pltpu.VMEM((seq_count, 2, rows, HD), bf),
            pltpu.VMEM((planes, rows, HD), bf),
            pltpu.VMEM((planes, rows, HD), bf),
            pltpu.VMEM((planes, rows, HD), bf),
            pltpu.VMEM((seq_count, LQ, width), bf),
            pltpu.VMEM((half, width), bf),
            pltpu.VMEM((half, width), bf),
            pltpu.VMEM((half, width), f32),
            pltpu.VMEM((2, half // 2, width), bf),
            pltpu.VMEM((2, half // 2, width), bf),
            pltpu.VMEM((rows, width), bf),
            pltpu.VMEM((rows, slots), f32),
            pltpu.VMEM((seq_count, groups, slots), f32),
            pltpu.VMEM((seq_count, 8, 128), f32),
            pltpu.VMEM((pb_count, 8, 128), f32),
            pltpu.SemaphoreType.DMA((4,)),
            pltpu.SemaphoreType.DMA,
            pltpu.SemaphoreType.DMA((copies,)),
            pltpu.SemaphoreType.DMA((copies,)),
        ],
        compiler_params=pltpu.CompilerParams(
            collective_id=0, has_side_effects=True, vmem_limit_bytes=56 * 1024 * 1024
        ),
    )(
        query_lengths,
        group_lengths,
        tokens,
        gain_attn.reshape(1, width),
        gain_embed.reshape(1, width),
        queries,
        teacher,
        w_key,
        w_value,
        w_query,
        w_out,
    )
    return embedded, scores, grad, loss.reshape(())


def run(*args):
    planes = args[1].shape[1] // HD
    fits = lax.axis_size("seq") == 2 * planes and lax.axis_size("pb") == 4 and args[7].shape[0] == 1
    return fused(*args) if fits else per_device(*args)


def solution(mesh):
    placed = (
        P("seq", None),
        P(None, "pb"),
        P(None, "pb"),
        P(None, "pb"),
        P("pb", None),
        P(),
        P(),
        P(("seq", "pb"), None, None),
        P(("seq", "pb")),
        P(),
        P(("seq", "pb"), None),
    )
    return jax.shard_map(
        run,
        mesh=mesh,
        in_specs=placed,
        out_specs=(P("seq", None), P(("seq", "pb"), None), P(("seq", "pb"), None), P()),
        check_vma=False,
    )
```

```python
import functools

import jax
import jax.numpy as jnp
from jax import lax
from jax.experimental import pallas as pl
from jax.experimental.pallas import tpu as pltpu
from jax.sharding import PartitionSpec as P

HD = 128
HEADS = 16
WIN = 2048
LQ = 32


EPSILON = 1e-06
SOFTMAX_TEMP = 0.1


def shifted_2(x, axis, by):
    count = lax.axis_size(axis)
    pairs = [(i, i + by) for i in range(count) if 0 <= i + by < count]
    return lax.ppermute(x, axis, pairs)


def rms_scale(values, gain):
    mean_sq = jnp.mean(values * values, axis=-1, keepdims=True)
    return values * lax.rsqrt(mean_sq + EPSILON) * gain


def segmented_max(values, group_id):
    span_len = values.shape[-1]
    stride = 1
    while stride < span_len:
        filler = jnp.full(values.shape[:-1] + (stride,), -jnp.inf, values.dtype)
        shifted = jnp.concatenate([filler, values[..., :-stride]], axis=-1)
        prior_id = jnp.concatenate([jnp.full((stride,), -1, jnp.int32), group_id[:-stride]])
        values = jnp.where((prior_id == group_id)[None, :], jnp.maximum(values, shifted), values)
        stride = stride * 2
    return values


def per_device(
    tokens,
    w_query,
    w_key,
    w_value,
    w_out,
    gain_attn,
    gain_embed,
    queries,
    query_lengths,
    group_lengths,
    teacher,
):
    shard_rows = tokens.shape[0]
    seq_count = lax.axis_size("seq")
    seq_place = lax.axis_index("seq")
    head_width = w_query.shape[1]
    heads_here = head_width // HD
    half_win = WIN // 2
    reach_count = half_win // shard_rows
    my_start = seq_place * shard_rows
    total_tokens = shard_rows * seq_count
    residual = tokens.astype(jnp.float32)
    normed = rms_scale(residual, gain_attn).astype(jnp.bfloat16)
    q_local = jnp.dot(normed, w_query, preferred_element_type=jnp.float32).astype(jnp.bfloat16)
    k_local = jnp.dot(normed, w_key, preferred_element_type=jnp.float32).astype(jnp.bfloat16)
    v_local = jnp.dot(normed, w_value, preferred_element_type=jnp.float32).astype(jnp.bfloat16)
    key_value = jnp.stack([k_local, v_local])
    earlier = [shifted_2(key_value, "seq", distance) for distance in range(reach_count, 0, -1)]
    later = [shifted_2(key_value, "seq", -distance) for distance in range(1, reach_count + 1)]
    window = jnp.concatenate(earlier + [key_value] + later, axis=1)
    span_rows = window.shape[1]
    q_pos = my_start + jnp.arange(shard_rows, dtype=jnp.int32)
    k_pos = my_start - reach_count * shard_rows + jnp.arange(span_rows, dtype=jnp.int32)
    in_window = (
        (jnp.abs(q_pos[:, None] - k_pos[None, :]) <= half_win)
        & (k_pos >= 0)[None, :]
        & (k_pos < total_tokens)[None, :]
    )
    q_heads = q_local.reshape(shard_rows, heads_here, HD)
    k_heads = window[0].reshape(span_rows, heads_here, HD)
    v_heads = window[1].reshape(span_rows, heads_here, HD)
    logits = jnp.einsum(
        "qhd,khd->hqk", q_heads, k_heads, preferred_element_type=jnp.float32
    ) * HD ** (-0.5)
    logits = jnp.where(in_window[None], logits, -jnp.inf)
    row_max = jnp.max(logits, axis=-1, keepdims=True)
    exp_terms = jnp.exp(logits - row_max)
    weights = (exp_terms / jnp.sum(exp_terms, axis=-1, keepdims=True)).astype(jnp.bfloat16)
    mixed = jnp.einsum("hqk,khd->qhd", weights, v_heads, preferred_element_type=jnp.float32)
    mixed = mixed.reshape(shard_rows, head_width).astype(jnp.bfloat16)
    partial_value = jnp.dot(mixed, w_out, preferred_element_type=jnp.float32)
    attn_sum = lax.psum(partial_value, "pb")
    embedded = rms_scale(residual + attn_sum, gain_embed).astype(jnp.bfloat16)
    group_end = jnp.cumsum(group_lengths)
    group_start = group_end - group_lengths
    group_id = jnp.sum((group_end[None, :] <= q_pos[:, None]).astype(jnp.int32), axis=1)
    last_local = jnp.clip(group_end - 1 - my_start, 0, shard_rows - 1)
    present = (group_start < my_start + shard_rows) & (group_end > my_start)
    q_piece = lax.all_gather(queries, "seq", axis=0, tiled=True)
    count = q_piece.shape[0]
    q_rows = q_piece.reshape(count * q_piece.shape[1], q_piece.shape[2])
    similar = jnp.einsum("td,rd->tr", q_rows, embedded, preferred_element_type=jnp.float32)
    running = segmented_max(similar, group_id)
    picked = jnp.take(running, last_local, axis=1)
    picked = jnp.where(present[None, :], picked, -jnp.inf)
    part_max = picked.reshape(count, q_piece.shape[1], picked.shape[-1])
    own_count = queries.shape[0]
    all_maxima = lax.pmax(part_max, "seq")
    token_max = lax.dynamic_slice_in_dim(all_maxima, seq_place * own_count, own_count, 0)
    live_mask = (jnp.arange(LQ, dtype=jnp.int32)[None, :] < query_lengths[:, None]).astype(
        jnp.float32
    )
    scores = (
        jnp.sum(token_max * live_mask[:, :, None], axis=1)
        / query_lengths.astype(jnp.float32)[:, None]
    )
    student_scores = scores / SOFTMAX_TEMP
    student_scores = student_scores - jnp.max(student_scores, axis=-1, keepdims=True)
    student_log_prob = student_scores - jnp.log(
        jnp.sum(jnp.exp(student_scores), axis=-1, keepdims=True)
    )
    target_scores = teacher / SOFTMAX_TEMP
    target_scores = target_scores - jnp.max(target_scores, axis=-1, keepdims=True)
    log_t = target_scores - jnp.log(jnp.sum(jnp.exp(target_scores), axis=-1, keepdims=True))
    teacher_prob = jnp.exp(log_t)
    kl_terms = jnp.sum(teacher_prob * (log_t - student_log_prob), axis=-1)
    query_count_all = own_count * seq_count * lax.axis_size("pb")
    distill_loss = lax.psum(jnp.sum(kl_terms), ("seq", "pb")) / query_count_all
    score_gradient = (jnp.exp(student_log_prob) - teacher_prob) / (SOFTMAX_TEMP * query_count_all)
    return (embedded, scores, score_gradient, distill_loss)


MESH = pl.DeviceIdType.MESH
NEG = float("-inf")


def fused_kernel(
    seq_count,
    pb_count,
    lengths_ref,
    groups_ref,
    tokens_ref,
    gain_attn_ref,
    gain_embed_ref,
    queries_ref,
    teacher_ref,
    wk_hbm,
    wv_hbm,
    wq_hbm,
    wo_hbm,
    emb_hbm,
    scores_ref,
    grad_ref,
    loss_ref,
    wk,
    wv,
    wq,
    wo,
    kv_send,
    q_send,
    kv,
    q_in,
    m_send,
    m_in,
    query_all,
    a_send,
    a_in,
    own_sum,
    emb,
    sim,
    gmax,
    kl_seq,
    kl_pb,
    w_sem,
    out_sem,
    send,
    recv,
):
    me = lax.axis_index("seq")
    pb = lax.axis_index("pb")
    planes = seq_count // 2
    z, y = me // 2, lax.rem(me, 2)
    core, x = lax.rem(pb, 2), pb // 2
    core_mate = pb + 1 - 2 * core
    x_mate = lax.rem(pb + 2, pb_count)
    y_mate = me + 1 - 2 * y
    rows = tokens_ref.shape[0]
    half = rows // 2
    chunk = half // 2
    own_rows = pl.multiple_of(core * half, half)
    mate_rows = pl.multiple_of((1 - core) * half, half)
    groups = groups_ref.shape[0]

    QU, QD, QY, KZ, KY, TQ, MX, XX = (i * planes for i in range(8))
    CA, WX, CD = 8 * planes, 8 * planes + 1, 8 * planes + 2
    GM = 8 * planes + 4
    LS, LP = GM + seq_count, GM + 2 * seq_count

    def remote(src, dst, out_place, in_place, where):
        return pltpu.make_async_remote_copy(
            src_ref=src,
            dst_ref=dst,
            send_sem=send.at[out_place],
            recv_sem=recv.at[in_place],
            device_id=where,
            device_id_type=MESH,
        )

    loads = [
        pltpu.make_async_copy(src, dst, w_sem.at[i])
        for i, (src, dst) in enumerate(((wk_hbm, wk), (wv_hbm, wv), (wq_hbm, wq), (wo_hbm, wo.at[x])))
    ]
    for load in loads:
        load.start()

    barrier = pltpu.get_barrier_semaphore()
    for d in range(1, seq_count):
        pl.semaphore_signal(
            barrier,
            inc=1,
            device_id={"seq": lax.rem(me + d, seq_count)},
            device_id_type=MESH,
        )
    for d in range(1, pb_count):
        pl.semaphore_signal(
            barrier,
            inc=1,
            device_id={"pb": lax.rem(pb + d, pb_count)},
            device_id_type=MESH,
        )
    query_all[me] = queries_ref[0]
    residual = tokens_ref[...].astype(jnp.float32)
    normed = rms_scale(residual, gain_attn_ref[...]).astype(jnp.bfloat16)
    pl.semaphore_wait(barrier, seq_count + pb_count - 2)

    def along(d):
        return lax.rem(z + d, planes)

    sent = []

    def go(copy):
        copy.start()
        sent.append(copy)

    go(remote(wo_hbm, wo.at[x], WX, WX, {"pb": x_mate}))

    def hop(far):
        upward, downward = 2 * (z - far) + y, 2 * (z + far) + y
        up = remote(query_all.at[upward], query_all.at[upward], QU + z - far, QU + z - far, {"seq": me + 2})
        down = remote(query_all.at[downward], query_all.at[downward], QD + z + far, QD + z + far, {"seq": me - 2})
        return ((z >= far) & (z < planes - 1), up), ((z + far < planes) & (z > 0), down)

    def hop_in(far):
        for sign in (-1, 1):
            source = z + sign * far
            slot = 2 * source + y

            @pl.when((source >= 0) & (source < planes))
            def _():
                block = query_all.at[slot]
                place = (QU if sign < 0 else QD) + source
                remote(block, block, place, place, {"seq": me + 2 * sign}).wait_recv()

    def hop_out(far):
        for valid, copy in hop(far):
            pl.when(valid)(copy.start)
        for sign in (-1, 1) if far else (1,):
            source = z + sign * far
            slot = 2 * source + y

            @pl.when((source >= 0) & (source < planes))
            def _():
                block = query_all.at[slot]
                remote(block, block, QY + source, QY + source, {"seq": y_mate}).start()

    hop_out(0)

    loads[0].wait()
    k_all = jnp.dot(normed, wk[...], preferred_element_type=jnp.float32).astype(jnp.bfloat16)
    for h in range(planes):
        kv_send[h, 0] = k_all[:, h * HD : (h + 1) * HD]
    loads[1].wait()
    v_all = jnp.dot(normed, wv[...], preferred_element_type=jnp.float32).astype(jnp.bfloat16)
    for h in range(planes):
        kv_send[h, 1] = v_all[:, h * HD : (h + 1) * HD]
    for d in range(1, planes):
        other = along(d)
        go(remote(kv_send.at[other], kv.at[me], KZ + other, KZ + z, {"seq": 2 * other + y}))
    kv[me] = kv_send[z]
    go(remote(kv.at[me], kv.at[me], KY + z, KY + z, {"seq": y_mate}))
    loads[2].wait()
    q_all = jnp.dot(normed, wq[...], preferred_element_type=jnp.float32).astype(jnp.bfloat16)
    for h in range(planes):
        q_send[h] = q_all[:, h * HD : (h + 1) * HD]
    q_in[z] = q_send[z]

    for d in range(1, planes):
        source = along(planes - d)
        slot = 2 * source + y
        remote(kv.at[slot], kv.at[slot], KZ + source, KZ + source, {"seq": slot}).wait_recv()
        go(remote(kv.at[slot], kv.at[slot], KY + source, KY + source, {"seq": y_mate}))
    for d in range(1, planes):
        other = along(d)
        go(remote(q_send.at[other], q_in.at[z], TQ + other, TQ + z, {"seq": 2 * other + y}))
    for d in range(planes):
        source = along(planes - d)
        slot = 2 * source + 1 - y
        remote(kv.at[slot], kv.at[slot], KY + source, KY + source, {"seq": y_mate}).wait_recv()

    span = rows * seq_count
    gap = lax.broadcasted_iota(jnp.int32, (rows, span), 0) - lax.broadcasted_iota(
        jnp.int32, (rows, span), 1
    )

    def attend(source):
        base = (2 * source + y) * rows
        keys = kv[:, 0].reshape(span, HD)
        values = kv[:, 1].reshape(span, HD)
        logits = lax.dot_general(
            q_in[source], keys, (((1,), (1,)), ((), ())), preferred_element_type=jnp.float32
        )
        logits = jnp.where(jnp.abs(gap + base) <= WIN // 2, logits, NEG)
        row_max = jnp.max(logits, axis=-1, keepdims=True)
        terms = jnp.exp((logits - row_max) * HD ** (-0.5))
        total = jnp.sum(terms, axis=-1, keepdims=True)
        out = jnp.dot(terms.astype(jnp.bfloat16), values, preferred_element_type=jnp.float32)
        return (out / total).astype(jnp.bfloat16)

    def over(h):
        return remote(m_in.at[x, h], m_in.at[x, h], XX + h, XX + h, {"pb": x_mate})

    hop_in(1)
    hop_out(1)
    m_in[x, z] = attend(z)
    go(over(z))
    for d in range(1, planes):
        source = along(d)
        slot = 2 * source + y
        remote(q_in.at[source], q_in.at[source], TQ + source, TQ + source, {"seq": slot}).wait_recv()
        m_send[source] = attend(source)
        go(remote(m_send.at[source], m_in.at[x, z], MX + source, MX + z, {"seq": slot}))
        if d + 1 < planes:
            hop_in(d + 1)
            hop_out(d + 1)
    for d in range(1, planes):
        source = along(planes - d)
        block = m_in.at[x, source]
        remote(block, block, MX + source, MX + source, {"seq": 2 * source + y}).wait_recv()
        go(over(source))

    loads[3].wait()

    remote(wo.at[1 - x], wo.at[1 - x], WX, WX, {"pb": x_mate}).wait_recv()
    for h in range(planes):
        block = m_in.at[1 - x, h]
        remote(block, block, XX + h, XX + h, {"pb": x_mate}).wait_recv()

    def project(first):
        mixed = jnp.concatenate(
            [m_in[i, h, pl.ds(first, half), :] for i in range(2) for h in range(planes)], axis=1
        )
        weight = wo[...].reshape(2 * wo.shape[1], wo.shape[2])
        return jnp.dot(mixed, weight, preferred_element_type=jnp.float32)

    a_send[...] = project(mate_rows).astype(jnp.bfloat16)
    copy_a = remote(a_send, a_in, CA, CA, {"pb": core_mate})
    go(copy_a)
    own_sum[...] = project(own_rows)
    copy_a.wait_recv()
    for d in range(planes):
        source = along(planes - d)
        slot = 2 * source + 1 - y
        remote(query_all.at[slot], query_all.at[slot], QY + source, QY + source, {"seq": y_mate}).wait_recv()
    for i in range(2):
        here = pl.ds(pl.multiple_of(own_rows + i * chunk, chunk), chunk)
        part = slice(i * chunk, (i + 1) * chunk)
        attn = own_sum[part] + a_in[part].astype(jnp.float32)
        total = tokens_ref[here, :].astype(jnp.float32) + attn
        emb[here, :] = rms_scale(total, gain_embed_ref[...]).astype(jnp.bfloat16)
        go(remote(emb.at[here, :], emb.at[here, :], CD + i, CD + i, {"pb": core_mate}))

    q_rows = query_all[...].reshape(query_all.shape[0] * query_all.shape[1], query_all.shape[2])

    def compare(first):
        sim[pl.ds(first, half), :] = lax.dot_general(
            emb[pl.ds(first, half), :], q_rows, (((1,), (1,)), ((), ())), preferred_element_type=jnp.float32
        )

    compare(own_rows)
    for i in range(2):
        there = pl.ds(pl.multiple_of(mate_rows + i * chunk, chunk), chunk)
        remote(emb.at[there, :], emb.at[there, :], CD + i, CD + i, {"pb": core_mate}).wait_recv()
    store = pltpu.make_async_copy(emb, emb_hbm, out_sem)
    store.start()
    compare(mate_rows)

    similar = sim[...]
    position = lax.broadcasted_iota(jnp.int32, similar.shape, 0) + me * rows
    begin = jnp.int32(0)
    for c in range(groups):
        end = begin + groups_ref[c]
        inside = (position >= begin) & (position < end)
        gmax[me, c : c + 1] = jnp.max(jnp.where(inside, similar, NEG), axis=0, keepdims=True)
        begin = end
    for d in range(1, seq_count):
        other = lax.rem(me + d, seq_count)
        go(remote(gmax.at[me], gmax.at[me], GM + other, GM + me, {"seq": other}))
    for d in range(1, seq_count):
        other = lax.rem(me + d, seq_count)
        remote(gmax.at[other], gmax.at[other], GM + other, GM + other, {"seq": other}).wait_recv()
    token_max = jnp.max(gmax[...], axis=0)
    slot_of = lax.broadcasted_iota(jnp.int32, token_max.shape, 1) - me * LQ
    length = lengths_ref[0]
    live = (slot_of >= 0) & (slot_of < length)
    column = jnp.sum(jnp.where(live, token_max, 0.0), axis=1, keepdims=True)
    square = (groups, groups)
    diagonal = lax.broadcasted_iota(jnp.int32, square, 0) == lax.broadcasted_iota(jnp.int32, square, 1)
    row = jnp.sum(jnp.where(diagonal, column, 0.0), axis=0, keepdims=True)
    scores = row / length.astype(jnp.float32)
    scores_ref[...] = scores

    def log_softmax(values):
        values = values / SOFTMAX_TEMP
        values = values - jnp.max(values, axis=-1, keepdims=True)
        return values - jnp.log(jnp.sum(jnp.exp(values), axis=-1, keepdims=True))

    log_s = log_softmax(scores)
    log_t = log_softmax(teacher_ref[...])
    prob = jnp.exp(log_t)
    amount = seq_count * pb_count
    grad_ref[...] = (jnp.exp(log_s) - prob) / (SOFTMAX_TEMP * amount)
    kl = jnp.sum(prob * (log_t - log_s), axis=-1, keepdims=True)
    kl_seq[me] = jnp.broadcast_to(kl, kl_seq.shape[1:])
    for d in range(1, seq_count):
        other = lax.rem(me + d, seq_count)
        go(remote(kl_seq.at[me], kl_seq.at[me], LS + other, LS + me, {"seq": other}))
    for d in range(1, seq_count):
        other = lax.rem(me + d, seq_count)
        remote(kl_seq.at[other], kl_seq.at[other], LS + other, LS + other, {"seq": other}).wait_recv()
    kl_pb[pb] = jnp.sum(kl_seq[...], axis=0)
    for d in range(1, pb_count):
        other = lax.rem(pb + d, pb_count)
        go(remote(kl_pb.at[pb], kl_pb.at[pb], LP + other, LP + pb, {"pb": other}))
    for d in range(1, pb_count):
        other = lax.rem(pb + d, pb_count)
        remote(kl_pb.at[other], kl_pb.at[other], LP + other, LP + other, {"pb": other}).wait_recv()
    loss_ref[...] = jnp.sum(kl_pb[...], axis=0)[:1, :1] / amount

    for copy in sent:
        copy.wait_send()
    for far in range(planes):
        for valid, copy in hop(far):
            pl.when(valid)(copy.wait_send)
    for source in range(planes):
        block = query_all.at[2 * source + y]
        remote(block, block, QY + source, QY + source, {"seq": y_mate}).wait_send()
    store.wait()


def fused(
    tokens,
    w_query,
    w_key,
    w_value,
    w_out,
    gain_attn,
    gain_embed,
    queries,
    query_lengths,
    group_lengths,
    teacher,
):
    seq_count, pb_count = lax.axis_size("seq"), lax.axis_size("pb")
    rows, width = tokens.shape
    head_width = w_query.shape[1]
    planes = seq_count // 2
    groups = group_lengths.shape[0]
    slots = queries.shape[0] * seq_count * LQ
    half = rows // 2
    bf, f32 = jnp.bfloat16, jnp.float32
    vmem, smem = pl.BlockSpec(memory_space=pltpu.VMEM), pl.BlockSpec(memory_space=pltpu.SMEM)
    hbm = pl.BlockSpec(memory_space=pl.ANY)
    copies = 8 * planes + 4 + 2 * seq_count + pb_count
    embedded, scores, grad, loss = pl.pallas_call(
        functools.partial(fused_kernel, seq_count, pb_count),
        out_shape=(
            jax.ShapeDtypeStruct((rows, width), bf),
            jax.ShapeDtypeStruct((1, groups), f32),
            jax.ShapeDtypeStruct((1, groups), f32),
            jax.ShapeDtypeStruct((1, 1), f32),
        ),
        in_specs=[smem, smem] + [vmem] * 5 + [hbm] * 4,
        out_specs=(hbm, vmem, vmem, vmem),
        scratch_shapes=[
            pltpu.VMEM((width, head_width), bf),
            pltpu.VMEM((width, head_width), bf),
            pltpu.VMEM((width, head_width), bf),
            pltpu.VMEM((2, head_width, width), bf),
            pltpu.VMEM((planes, 2, rows, HD), bf),
            pltpu.VMEM((planes, rows, HD), bf),
            pltpu.VMEM((seq_count, 2, rows, HD), bf),
            pltpu.VMEM((planes, rows, HD), bf),
            pltpu.VMEM((planes, rows, HD), bf),
            pltpu.VMEM((2, planes, rows, HD), bf),
            pltpu.VMEM((seq_count, LQ, width), bf),
            pltpu.VMEM((half, width), bf),
            pltpu.VMEM((half, width), bf),
            pltpu.VMEM((half, width), f32),
            pltpu.VMEM((rows, width), bf),
            pltpu.VMEM((rows, slots), f32),
            pltpu.VMEM((seq_count, groups, slots), f32),
            pltpu.VMEM((seq_count, 8, 128), f32),
            pltpu.VMEM((pb_count, 8, 128), f32),
            pltpu.SemaphoreType.DMA((4,)),
            pltpu.SemaphoreType.DMA,
            pltpu.SemaphoreType.DMA((copies,)),
            pltpu.SemaphoreType.DMA((copies,)),
        ],
        compiler_params=pltpu.CompilerParams(
            collective_id=0, has_side_effects=True, vmem_limit_bytes=56 * 1024 * 1024
        ),
    )(
        query_lengths,
        group_lengths,
        tokens,
        gain_attn.reshape(1, width),
        gain_embed.reshape(1, width),
        queries,
        teacher,
        w_key,
        w_value,
        w_query,
        w_out,
    )
    return embedded, scores, grad, loss.reshape(())


def run(*args):
    planes = args[1].shape[1] // HD
    fits = lax.axis_size("seq") == 2 * planes and lax.axis_size("pb") == 4 and args[7].shape[0] == 1
    return fused(*args) if fits else per_device(*args)


def solution(mesh):
    placed = (
        P("seq", None),
        P(None, "pb"),
        P(None, "pb"),
        P(None, "pb"),
        P("pb", None),
        P(),
        P(),
        P(("seq", "pb"), None, None),
        P(("seq", "pb")),
        P(),
        P(("seq", "pb"), None),
    )
    return jax.shard_map(
        run,
        mesh=mesh,
        in_specs=placed,
        out_specs=(P("seq", None), P(("seq", "pb"), None), P(("seq", "pb"), None), P()),
        check_vma=False,
    )
```

```python
import functools

import jax
import jax.numpy as jnp
from jax import lax
from jax.experimental import pallas as pl
from jax.experimental.pallas import tpu as pltpu
from jax.sharding import PartitionSpec as P

HD = 128
HEADS = 16
WIN = 2048
LQ = 32


EPSILON = 1e-06
SOFTMAX_TEMP = 0.1


def shifted_2(x, axis, by):
    count = lax.axis_size(axis)
    pairs = [(i, i + by) for i in range(count) if 0 <= i + by < count]
    return lax.ppermute(x, axis, pairs)


def rms_scale(values, gain):
    mean_sq = jnp.mean(values * values, axis=-1, keepdims=True)
    return values * lax.rsqrt(mean_sq + EPSILON) * gain


def segmented_max(values, group_id):
    span_len = values.shape[-1]
    stride = 1
    while stride < span_len:
        filler = jnp.full(values.shape[:-1] + (stride,), -jnp.inf, values.dtype)
        shifted = jnp.concatenate([filler, values[..., :-stride]], axis=-1)
        prior_id = jnp.concatenate([jnp.full((stride,), -1, jnp.int32), group_id[:-stride]])
        values = jnp.where((prior_id == group_id)[None, :], jnp.maximum(values, shifted), values)
        stride = stride * 2
    return values


def per_device(
    tokens,
    w_query,
    w_key,
    w_value,
    w_out,
    gain_attn,
    gain_embed,
    queries,
    query_lengths,
    group_lengths,
    teacher,
):
    shard_rows = tokens.shape[0]
    seq_count = lax.axis_size("seq")
    seq_place = lax.axis_index("seq")
    head_width = w_query.shape[1]
    heads_here = head_width // HD
    half_win = WIN // 2
    reach_count = half_win // shard_rows
    my_start = seq_place * shard_rows
    total_tokens = shard_rows * seq_count
    residual = tokens.astype(jnp.float32)
    normed = rms_scale(residual, gain_attn).astype(jnp.bfloat16)
    q_local = jnp.dot(normed, w_query, preferred_element_type=jnp.float32).astype(jnp.bfloat16)
    k_local = jnp.dot(normed, w_key, preferred_element_type=jnp.float32).astype(jnp.bfloat16)
    v_local = jnp.dot(normed, w_value, preferred_element_type=jnp.float32).astype(jnp.bfloat16)
    key_value = jnp.stack([k_local, v_local])
    earlier = [shifted_2(key_value, "seq", distance) for distance in range(reach_count, 0, -1)]
    later = [shifted_2(key_value, "seq", -distance) for distance in range(1, reach_count + 1)]
    window = jnp.concatenate(earlier + [key_value] + later, axis=1)
    span_rows = window.shape[1]
    q_pos = my_start + jnp.arange(shard_rows, dtype=jnp.int32)
    k_pos = my_start - reach_count * shard_rows + jnp.arange(span_rows, dtype=jnp.int32)
    in_window = (
        (jnp.abs(q_pos[:, None] - k_pos[None, :]) <= half_win)
        & (k_pos >= 0)[None, :]
        & (k_pos < total_tokens)[None, :]
    )
    q_heads = q_local.reshape(shard_rows, heads_here, HD)
    k_heads = window[0].reshape(span_rows, heads_here, HD)
    v_heads = window[1].reshape(span_rows, heads_here, HD)
    logits = jnp.einsum(
        "qhd,khd->hqk", q_heads, k_heads, preferred_element_type=jnp.float32
    ) * HD ** (-0.5)
    logits = jnp.where(in_window[None], logits, -jnp.inf)
    row_max = jnp.max(logits, axis=-1, keepdims=True)
    exp_terms = jnp.exp(logits - row_max)
    weights = (exp_terms / jnp.sum(exp_terms, axis=-1, keepdims=True)).astype(jnp.bfloat16)
    mixed = jnp.einsum("hqk,khd->qhd", weights, v_heads, preferred_element_type=jnp.float32)
    mixed = mixed.reshape(shard_rows, head_width).astype(jnp.bfloat16)
    partial_value = jnp.dot(mixed, w_out, preferred_element_type=jnp.float32)
    attn_sum = lax.psum(partial_value, "pb")
    embedded = rms_scale(residual + attn_sum, gain_embed).astype(jnp.bfloat16)
    group_end = jnp.cumsum(group_lengths)
    group_start = group_end - group_lengths
    group_id = jnp.sum((group_end[None, :] <= q_pos[:, None]).astype(jnp.int32), axis=1)
    last_local = jnp.clip(group_end - 1 - my_start, 0, shard_rows - 1)
    present = (group_start < my_start + shard_rows) & (group_end > my_start)
    q_piece = lax.all_gather(queries, "seq", axis=0, tiled=True)
    count = q_piece.shape[0]
    q_rows = q_piece.reshape(count * q_piece.shape[1], q_piece.shape[2])
    similar = jnp.einsum("td,rd->tr", q_rows, embedded, preferred_element_type=jnp.float32)
    running = segmented_max(similar, group_id)
    picked = jnp.take(running, last_local, axis=1)
    picked = jnp.where(present[None, :], picked, -jnp.inf)
    part_max = picked.reshape(count, q_piece.shape[1], picked.shape[-1])
    own_count = queries.shape[0]
    all_maxima = lax.pmax(part_max, "seq")
    token_max = lax.dynamic_slice_in_dim(all_maxima, seq_place * own_count, own_count, 0)
    live_mask = (jnp.arange(LQ, dtype=jnp.int32)[None, :] < query_lengths[:, None]).astype(
        jnp.float32
    )
    scores = (
        jnp.sum(token_max * live_mask[:, :, None], axis=1)
        / query_lengths.astype(jnp.float32)[:, None]
    )
    student_scores = scores / SOFTMAX_TEMP
    student_scores = student_scores - jnp.max(student_scores, axis=-1, keepdims=True)
    student_log_prob = student_scores - jnp.log(
        jnp.sum(jnp.exp(student_scores), axis=-1, keepdims=True)
    )
    target_scores = teacher / SOFTMAX_TEMP
    target_scores = target_scores - jnp.max(target_scores, axis=-1, keepdims=True)
    log_t = target_scores - jnp.log(jnp.sum(jnp.exp(target_scores), axis=-1, keepdims=True))
    teacher_prob = jnp.exp(log_t)
    kl_terms = jnp.sum(teacher_prob * (log_t - student_log_prob), axis=-1)
    query_count_all = own_count * seq_count * lax.axis_size("pb")
    distill_loss = lax.psum(jnp.sum(kl_terms), ("seq", "pb")) / query_count_all
    score_gradient = (jnp.exp(student_log_prob) - teacher_prob) / (SOFTMAX_TEMP * query_count_all)
    return (embedded, scores, score_gradient, distill_loss)


MESH = pl.DeviceIdType.MESH
NEG = float("-inf")


def fused_kernel(
    seq_count,
    pb_count,
    lengths_ref,
    groups_ref,
    tokens_ref,
    gain_attn_ref,
    gain_embed_ref,
    queries_ref,
    teacher_ref,
    wk_hbm,
    wv_hbm,
    wq_hbm,
    wo_hbm,
    emb_ref,
    scores_ref,
    grad_ref,
    loss_ref,
    wk,
    wv,
    wq,
    wo,
    kv_send,
    q_send,
    kv,
    q_in,
    m_send,
    m_in,
    query_all,
    a_send,
    a_in,
    own_sum,
    emb,
    sim,
    gmax,
    kl_seq,
    kl_pb,
    w_sem,
    out_sem,
    send,
    recv,
):
    me = lax.axis_index("seq")
    pb = lax.axis_index("pb")
    planes = seq_count // 2
    z, y = me // 2, lax.rem(me, 2)
    core, x = lax.rem(pb, 2), pb // 2
    core_mate = pb + 1 - 2 * core
    x_mate = lax.rem(pb + 2, pb_count)
    y_mate = me + 1 - 2 * y
    rows = tokens_ref.shape[0]
    half = rows // 2
    chunk = half // 2
    own_rows = pl.multiple_of(core * half, half)
    mate_rows = pl.multiple_of((1 - core) * half, half)
    groups = groups_ref.shape[0]

    QU, QD, QY, KZ, KY, TQ, MX, XX = (i * planes for i in range(8))
    CA, CD, WX = 8 * planes, 8 * planes + 1, 8 * planes + 3
    WY = WX + planes - 1
    GM = WY + 1
    LS, LP = GM + seq_count, GM + 2 * seq_count

    def remote(src, dst, out_place, in_place, where):
        return pltpu.make_async_remote_copy(
            src_ref=src,
            dst_ref=dst,
            send_sem=send.at[out_place],
            recv_sem=recv.at[in_place],
            device_id=where,
            device_id_type=MESH,
        )

    loads = [
        pltpu.make_async_copy(src, dst, w_sem.at[i])
        for i, (src, dst) in enumerate(((wk_hbm, wk), (wv_hbm, wv), (wq_hbm, wq), (wo_hbm, wo.at[x])))
    ]
    for load in loads:
        load.start()

    barrier = pltpu.get_barrier_semaphore()
    for d in range(1, seq_count):
        pl.semaphore_signal(
            barrier,
            inc=1,
            device_id={"seq": lax.rem(me + d, seq_count)},
            device_id_type=MESH,
        )
    for d in range(1, pb_count):
        pl.semaphore_signal(
            barrier,
            inc=1,
            device_id={"pb": lax.rem(pb + d, pb_count)},
            device_id_type=MESH,
        )
    query_all[me] = queries_ref[0]
    residual = tokens_ref[...].astype(jnp.float32)
    normed = rms_scale(residual, gain_attn_ref[...]).astype(jnp.bfloat16)
    pl.semaphore_wait(barrier, seq_count + pb_count - 2)

    def along(d):
        return lax.rem(z + d, planes)

    sent = []

    def go(copy):
        copy.start()
        sent.append(copy)

    def wanted(i):
        return y * (planes - 1) + (1 - 2 * y) * i

    def fetch(i):
        h = wanted(i)
        return remote(wo_hbm.at[h], wo.at[x, h], WX + i, WX + i, {"pb": x_mate})

    def fetched(i):
        block = wo.at[1 - x, wanted(i)]
        remote(block, block, WX + i, WX + i, {"pb": x_mate}).wait_recv()

    for i in range(planes - 2):
        go(fetch(i))

    def hop(far):
        upward, downward = 2 * (z - far) + y, 2 * (z + far) + y
        up = remote(query_all.at[upward], query_all.at[upward], QU + z - far, QU + z - far, {"seq": me + 2})
        down = remote(query_all.at[downward], query_all.at[downward], QD + z + far, QD + z + far, {"seq": me - 2})
        return ((z >= far) & (z < planes - 1), up), ((z + far < planes) & (z > 0), down)

    def hop_in(far):
        for sign in (-1, 1):
            source = z + sign * far
            slot = 2 * source + y

            @pl.when((source >= 0) & (source < planes))
            def _():
                block = query_all.at[slot]
                place = (QU if sign < 0 else QD) + source
                remote(block, block, place, place, {"seq": me + 2 * sign}).wait_recv()

    def hop_out(far):
        for valid, copy in hop(far):
            pl.when(valid)(copy.start)
        for sign in (-1, 1) if far else (1,):
            source = z + sign * far
            slot = 2 * source + y

            @pl.when((source >= 0) & (source < planes))
            def _():
                block = query_all.at[slot]
                remote(block, block, QY + source, QY + source, {"seq": y_mate}).start()

    hop_out(0)

    loads[0].wait()
    k_all = jnp.dot(normed, wk[...], preferred_element_type=jnp.float32).astype(jnp.bfloat16)
    for h in range(planes):
        kv_send[h, 0] = k_all[:, h * HD : (h + 1) * HD]
    loads[1].wait()
    v_all = jnp.dot(normed, wv[...], preferred_element_type=jnp.float32).astype(jnp.bfloat16)
    for h in range(planes):
        kv_send[h, 1] = v_all[:, h * HD : (h + 1) * HD]
    for d in range(1, planes):
        other = along(d)
        go(remote(kv_send.at[other], kv.at[me], KZ + other, KZ + z, {"seq": 2 * other + y}))
    kv[me] = kv_send[z]
    go(remote(kv.at[me], kv.at[me], KY + z, KY + z, {"seq": y_mate}))
    loads[2].wait()
    q_all = jnp.dot(normed, wq[...], preferred_element_type=jnp.float32).astype(jnp.bfloat16)
    for h in range(planes):
        q_send[h] = q_all[:, h * HD : (h + 1) * HD]
    q_in[z] = q_send[z]

    for d in range(1, planes):
        source = along(planes - d)
        slot = 2 * source + y
        remote(kv.at[slot], kv.at[slot], KZ + source, KZ + source, {"seq": slot}).wait_recv()
        go(remote(kv.at[slot], kv.at[slot], KY + source, KY + source, {"seq": y_mate}))
    for d in range(1, planes):
        other = along(d)
        go(remote(q_send.at[other], q_in.at[z], TQ + other, TQ + z, {"seq": 2 * other + y}))
    for d in range(planes):
        source = along(planes - d)
        slot = 2 * source + 1 - y
        remote(kv.at[slot], kv.at[slot], KY + source, KY + source, {"seq": y_mate}).wait_recv()

    span = rows * seq_count
    key_at = lax.broadcasted_iota(jnp.int32, (1, span), 1)
    row_at = lax.broadcasted_iota(jnp.int32, (rows, 1), 0)

    def attend(source):
        query_at = row_at + (2 * source + y) * rows
        seen = (key_at >= query_at - WIN // 2) & (key_at <= query_at + WIN // 2)
        keys = kv[:, 0].reshape(span, HD)
        values = kv[:, 1].reshape(span, HD)
        logits = lax.dot_general(
            q_in[source], keys, (((1,), (1,)), ((), ())), preferred_element_type=jnp.float32
        )
        logits = jnp.where(seen, logits, NEG)
        row_max = jnp.max(logits, axis=-1, keepdims=True)
        terms = jnp.exp((logits - row_max) * HD ** (-0.5))
        total = jnp.sum(terms, axis=-1, keepdims=True)
        out = jnp.dot(terms.astype(jnp.bfloat16), values, preferred_element_type=jnp.float32)
        return (out / total).astype(jnp.bfloat16)

    def over(h):
        return remote(m_in.at[x, h], m_in.at[x, h], XX + h, XX + h, {"pb": x_mate})

    go(fetch(planes - 2))
    fetched(0)
    first = wo.at[1 - x, wanted(0)]
    go(remote(first, first, WY, WY, {"seq": y_mate}))
    hop_in(1)
    hop_out(1)
    m_in[x, z] = attend(z)
    go(over(z))
    for d in range(1, planes):
        source = along(d)
        slot = 2 * source + y
        remote(q_in.at[source], q_in.at[source], TQ + source, TQ + source, {"seq": slot}).wait_recv()
        m_send[source] = attend(source)
        go(remote(m_send.at[source], m_in.at[x, z], MX + source, MX + z, {"seq": slot}))
        if d + 1 < planes:
            hop_in(d + 1)
            hop_out(d + 1)
    for d in range(1, planes):
        source = along(planes - d)
        block = m_in.at[x, source]
        remote(block, block, MX + source, MX + source, {"seq": 2 * source + y}).wait_recv()
        go(over(source))

    loads[3].wait()

    for i in range(1, planes - 1):
        fetched(i)
    last = wo.at[1 - x, wanted(planes - 1)]
    remote(last, last, WY, WY, {"seq": y_mate}).wait_recv()
    for h in range(planes):
        block = m_in.at[1 - x, h]
        remote(block, block, XX + h, XX + h, {"pb": x_mate}).wait_recv()

    def project(first):
        mixed = jnp.concatenate(
            [m_in[i, h, pl.ds(first, half), :] for i in range(2) for h in range(planes)], axis=1
        )
        weight = wo[...].reshape(2 * planes * HD, wo.shape[3])
        return jnp.dot(mixed, weight, preferred_element_type=jnp.float32)

    a_send[...] = project(mate_rows).astype(jnp.bfloat16)
    copy_a = remote(a_send, a_in, CA, CA, {"pb": core_mate})
    go(copy_a)
    own_sum[...] = project(own_rows)
    copy_a.wait_recv()
    for d in range(planes):
        source = along(planes - d)
        slot = 2 * source + 1 - y
        remote(query_all.at[slot], query_all.at[slot], QY + source, QY + source, {"seq": y_mate}).wait_recv()
    for i in range(2):
        here = pl.ds(pl.multiple_of(own_rows + i * chunk, chunk), chunk)
        part = slice(i * chunk, (i + 1) * chunk)
        attn = own_sum[part] + a_in[part].astype(jnp.float32)
        total = tokens_ref[here, :].astype(jnp.float32) + attn
        emb[here, :] = rms_scale(total, gain_embed_ref[...]).astype(jnp.bfloat16)
        go(remote(emb.at[here, :], emb.at[here, :], CD + i, CD + i, {"pb": core_mate}))

    q_rows = query_all[...].reshape(query_all.shape[0] * query_all.shape[1], query_all.shape[2])

    def compare(first):
        sim[pl.ds(first, half), :] = lax.dot_general(
            emb[pl.ds(first, half), :], q_rows, (((1,), (1,)), ((), ())), preferred_element_type=jnp.float32
        )

    compare(own_rows)
    for i in range(2):
        there = pl.ds(pl.multiple_of(mate_rows + i * chunk, chunk), chunk)
        remote(emb.at[there, :], emb.at[there, :], CD + i, CD + i, {"pb": core_mate}).wait_recv()
    store = pltpu.make_async_copy(emb, emb_ref, out_sem)
    store.start()
    compare(mate_rows)

    similar = sim[...]
    position = lax.broadcasted_iota(jnp.int32, similar.shape, 0) + me * rows
    begin = jnp.int32(0)
    for c in range(groups):
        end = begin + groups_ref[c]
        inside = (position >= begin) & (position < end)
        gmax[me, c : c + 1] = jnp.max(jnp.where(inside, similar, NEG), axis=0, keepdims=True)
        begin = end
    for d in range(1, seq_count):
        other = lax.rem(me + d, seq_count)
        go(remote(gmax.at[me], gmax.at[me], GM + other, GM + me, {"seq": other}))
    for d in range(1, seq_count):
        other = lax.rem(me + d, seq_count)
        remote(gmax.at[other], gmax.at[other], GM + other, GM + other, {"seq": other}).wait_recv()
    token_max = jnp.max(gmax[...], axis=0)
    slot_of = lax.broadcasted_iota(jnp.int32, token_max.shape, 1) - me * LQ
    length = lengths_ref[0]
    live = (slot_of >= 0) & (slot_of < length)
    column = jnp.sum(jnp.where(live, token_max, 0.0), axis=1, keepdims=True)
    square = (groups, groups)
    diagonal = lax.broadcasted_iota(jnp.int32, square, 0) == lax.broadcasted_iota(jnp.int32, square, 1)
    row = jnp.sum(jnp.where(diagonal, column, 0.0), axis=0, keepdims=True)
    scores = row / length.astype(jnp.float32)
    scores_ref[...] = scores

    def log_softmax(values):
        values = values / SOFTMAX_TEMP
        values = values - jnp.max(values, axis=-1, keepdims=True)
        return values - jnp.log(jnp.sum(jnp.exp(values), axis=-1, keepdims=True))

    log_s = log_softmax(scores)
    log_t = log_softmax(teacher_ref[...])
    prob = jnp.exp(log_t)
    amount = seq_count * pb_count
    grad_ref[...] = (jnp.exp(log_s) - prob) / (SOFTMAX_TEMP * amount)
    kl = jnp.sum(prob * (log_t - log_s), axis=-1, keepdims=True)
    kl_seq[me] = jnp.broadcast_to(kl, kl_seq.shape[1:])
    for d in range(1, seq_count):
        other = lax.rem(me + d, seq_count)
        go(remote(kl_seq.at[me], kl_seq.at[me], LS + other, LS + me, {"seq": other}))
    for d in range(1, seq_count):
        other = lax.rem(me + d, seq_count)
        remote(kl_seq.at[other], kl_seq.at[other], LS + other, LS + other, {"seq": other}).wait_recv()
    kl_pb[pb] = jnp.sum(kl_seq[...], axis=0)
    for d in range(1, pb_count):
        other = lax.rem(pb + d, pb_count)
        go(remote(kl_pb.at[pb], kl_pb.at[pb], LP + other, LP + pb, {"pb": other}))
    for d in range(1, pb_count):
        other = lax.rem(pb + d, pb_count)
        remote(kl_pb.at[other], kl_pb.at[other], LP + other, LP + other, {"pb": other}).wait_recv()
    loss_ref[...] = jnp.sum(kl_pb[...], axis=0)[:1, :1] / amount

    for copy in sent:
        copy.wait_send()
    for far in range(planes):
        for valid, copy in hop(far):
            pl.when(valid)(copy.wait_send)
    for source in range(planes):
        block = query_all.at[2 * source + y]
        remote(block, block, QY + source, QY + source, {"seq": y_mate}).wait_send()
    store.wait()


def fused(
    tokens,
    w_query,
    w_key,
    w_value,
    w_out,
    gain_attn,
    gain_embed,
    queries,
    query_lengths,
    group_lengths,
    teacher,
):
    seq_count, pb_count = lax.axis_size("seq"), lax.axis_size("pb")
    rows, width = tokens.shape
    head_width = w_query.shape[1]
    planes = seq_count // 2
    groups = group_lengths.shape[0]
    slots = queries.shape[0] * seq_count * LQ
    half = rows // 2
    bf, f32 = jnp.bfloat16, jnp.float32
    vmem, smem = pl.BlockSpec(memory_space=pltpu.VMEM), pl.BlockSpec(memory_space=pltpu.SMEM)
    hbm = pl.BlockSpec(memory_space=pl.ANY)
    copies = 9 * planes + 3 + 2 * seq_count + pb_count
    embedded, scores, grad, loss = pl.pallas_call(
        functools.partial(fused_kernel, seq_count, pb_count),
        out_shape=(
            pltpu.VMEM((rows, width), bf),
            jax.ShapeDtypeStruct((1, groups), f32),
            jax.ShapeDtypeStruct((1, groups), f32),
            jax.ShapeDtypeStruct((1, 1), f32),
        ),
        in_specs=[smem, smem] + [vmem] * 5 + [hbm] * 4,
        out_specs=(vmem, vmem, vmem, vmem),
        scratch_shapes=[
            pltpu.VMEM((width, head_width), bf),
            pltpu.VMEM((width, head_width), bf),
            pltpu.VMEM((width, head_width), bf),
            pltpu.VMEM((2, planes, HD, width), bf),
            pltpu.VMEM((planes, 2, rows, HD), bf),
            pltpu.VMEM((planes, rows, HD), bf),
            pltpu.VMEM((seq_count, 2, rows, HD), bf),
            pltpu.VMEM((planes, rows, HD), bf),
            pltpu.VMEM((planes, rows, HD), bf),
            pltpu.VMEM((2, planes, rows, HD), bf),
            pltpu.VMEM((seq_count, LQ, width), bf),
            pltpu.VMEM((half, width), bf),
            pltpu.VMEM((half, width), bf),
            pltpu.VMEM((half, width), f32),
            pltpu.VMEM((rows, width), bf),
            pltpu.VMEM((rows, slots), f32),
            pltpu.VMEM((seq_count, groups, slots), f32),
            pltpu.VMEM((seq_count, 8, 128), f32),
            pltpu.VMEM((pb_count, 8, 128), f32),
            pltpu.SemaphoreType.DMA((4,)),
            pltpu.SemaphoreType.DMA,
            pltpu.SemaphoreType.DMA((copies,)),
            pltpu.SemaphoreType.DMA((copies,)),
        ],
        compiler_params=pltpu.CompilerParams(
            collective_id=0, has_side_effects=True, vmem_limit_bytes=56 * 1024 * 1024
        ),
    )(
        query_lengths,
        group_lengths,
        tokens,
        gain_attn.reshape(1, width),
        gain_embed.reshape(1, width),
        queries,
        teacher,
        w_key,
        w_value,
        w_query,
        w_out.reshape(planes, HD, width),
    )
    return embedded, scores, grad, loss.reshape(())


def run(*args):
    planes = args[1].shape[1] // HD
    fits = lax.axis_size("seq") == 2 * planes and lax.axis_size("pb") == 4 and args[7].shape[0] == 1
    return fused(*args) if fits else per_device(*args)


def solution(mesh):
    placed = (
        P("seq", None),
        P(None, "pb"),
        P(None, "pb"),
        P(None, "pb"),
        P("pb", None),
        P(),
        P(),
        P(("seq", "pb"), None, None),
        P(("seq", "pb")),
        P(),
        P(("seq", "pb"), None),
    )
    return jax.shard_map(
        run,
        mesh=mesh,
        in_specs=placed,
        out_specs=(P("seq", None), P(("seq", "pb"), None), P(("seq", "pb"), None), P()),
        check_vma=False,
    )
```

```python
import functools
import math

import jax
import jax.numpy as jnp
from jax import lax
from jax.experimental import pallas as pl
from jax.experimental.pallas import tpu as pltpu
from jax.sharding import PartitionSpec as P

HD = 128
HEADS = 16
WIN = 2048
LQ = 32


EPSILON = 1e-06
SOFTMAX_TEMP = 0.1


def shifted_2(x, axis, by):
    count = lax.axis_size(axis)
    pairs = [(i, i + by) for i in range(count) if 0 <= i + by < count]
    return lax.ppermute(x, axis, pairs)


def rms_scale(values, gain):
    mean_sq = jnp.mean(values * values, axis=-1, keepdims=True)
    return values * lax.rsqrt(mean_sq + EPSILON) * gain


def segmented_max(values, group_id):
    span_len = values.shape[-1]
    stride = 1
    while stride < span_len:
        filler = jnp.full(values.shape[:-1] + (stride,), -jnp.inf, values.dtype)
        shifted = jnp.concatenate([filler, values[..., :-stride]], axis=-1)
        prior_id = jnp.concatenate([jnp.full((stride,), -1, jnp.int32), group_id[:-stride]])
        values = jnp.where((prior_id == group_id)[None, :], jnp.maximum(values, shifted), values)
        stride = stride * 2
    return values


def per_device(
    tokens,
    w_query,
    w_key,
    w_value,
    w_out,
    gain_attn,
    gain_embed,
    queries,
    query_lengths,
    group_lengths,
    teacher,
):
    shard_rows = tokens.shape[0]
    seq_count = lax.axis_size("seq")
    seq_place = lax.axis_index("seq")
    head_width = w_query.shape[1]
    heads_here = head_width // HD
    half_win = WIN // 2
    reach_count = half_win // shard_rows
    my_start = seq_place * shard_rows
    total_tokens = shard_rows * seq_count
    residual = tokens.astype(jnp.float32)
    normed = rms_scale(residual, gain_attn).astype(jnp.bfloat16)
    q_local = jnp.dot(normed, w_query, preferred_element_type=jnp.float32).astype(jnp.bfloat16)
    k_local = jnp.dot(normed, w_key, preferred_element_type=jnp.float32).astype(jnp.bfloat16)
    v_local = jnp.dot(normed, w_value, preferred_element_type=jnp.float32).astype(jnp.bfloat16)
    key_value = jnp.stack([k_local, v_local])
    earlier = [shifted_2(key_value, "seq", distance) for distance in range(reach_count, 0, -1)]
    later = [shifted_2(key_value, "seq", -distance) for distance in range(1, reach_count + 1)]
    window = jnp.concatenate(earlier + [key_value] + later, axis=1)
    span_rows = window.shape[1]
    q_pos = my_start + jnp.arange(shard_rows, dtype=jnp.int32)
    k_pos = my_start - reach_count * shard_rows + jnp.arange(span_rows, dtype=jnp.int32)
    in_window = (
        (jnp.abs(q_pos[:, None] - k_pos[None, :]) <= half_win)
        & (k_pos >= 0)[None, :]
        & (k_pos < total_tokens)[None, :]
    )
    q_heads = q_local.reshape(shard_rows, heads_here, HD)
    k_heads = window[0].reshape(span_rows, heads_here, HD)
    v_heads = window[1].reshape(span_rows, heads_here, HD)
    logits = jnp.einsum(
        "qhd,khd->hqk", q_heads, k_heads, preferred_element_type=jnp.float32
    ) * HD ** (-0.5)
    logits = jnp.where(in_window[None], logits, -jnp.inf)
    row_max = jnp.max(logits, axis=-1, keepdims=True)
    exp_terms = jnp.exp(logits - row_max)
    weights = (exp_terms / jnp.sum(exp_terms, axis=-1, keepdims=True)).astype(jnp.bfloat16)
    mixed = jnp.einsum("hqk,khd->qhd", weights, v_heads, preferred_element_type=jnp.float32)
    mixed = mixed.reshape(shard_rows, head_width).astype(jnp.bfloat16)
    partial_value = jnp.dot(mixed, w_out, preferred_element_type=jnp.float32)
    attn_sum = lax.psum(partial_value, "pb")
    embedded = rms_scale(residual + attn_sum, gain_embed).astype(jnp.bfloat16)
    group_end = jnp.cumsum(group_lengths)
    group_start = group_end - group_lengths
    group_id = jnp.sum((group_end[None, :] <= q_pos[:, None]).astype(jnp.int32), axis=1)
    last_local = jnp.clip(group_end - 1 - my_start, 0, shard_rows - 1)
    present = (group_start < my_start + shard_rows) & (group_end > my_start)
    q_piece = lax.all_gather(queries, "seq", axis=0, tiled=True)
    count = q_piece.shape[0]
    q_rows = q_piece.reshape(count * q_piece.shape[1], q_piece.shape[2])
    similar = jnp.einsum("td,rd->tr", q_rows, embedded, preferred_element_type=jnp.float32)
    running = segmented_max(similar, group_id)
    picked = jnp.take(running, last_local, axis=1)
    picked = jnp.where(present[None, :], picked, -jnp.inf)
    part_max = picked.reshape(count, q_piece.shape[1], picked.shape[-1])
    own_count = queries.shape[0]
    all_maxima = lax.pmax(part_max, "seq")
    token_max = lax.dynamic_slice_in_dim(all_maxima, seq_place * own_count, own_count, 0)
    live_mask = (jnp.arange(LQ, dtype=jnp.int32)[None, :] < query_lengths[:, None]).astype(
        jnp.float32
    )
    scores = (
        jnp.sum(token_max * live_mask[:, :, None], axis=1)
        / query_lengths.astype(jnp.float32)[:, None]
    )
    student_scores = scores / SOFTMAX_TEMP
    student_scores = student_scores - jnp.max(student_scores, axis=-1, keepdims=True)
    student_log_prob = student_scores - jnp.log(
        jnp.sum(jnp.exp(student_scores), axis=-1, keepdims=True)
    )
    target_scores = teacher / SOFTMAX_TEMP
    target_scores = target_scores - jnp.max(target_scores, axis=-1, keepdims=True)
    log_t = target_scores - jnp.log(jnp.sum(jnp.exp(target_scores), axis=-1, keepdims=True))
    teacher_prob = jnp.exp(log_t)
    kl_terms = jnp.sum(teacher_prob * (log_t - student_log_prob), axis=-1)
    query_count_all = own_count * seq_count * lax.axis_size("pb")
    distill_loss = lax.psum(jnp.sum(kl_terms), ("seq", "pb")) / query_count_all
    score_gradient = (jnp.exp(student_log_prob) - teacher_prob) / (SOFTMAX_TEMP * query_count_all)
    return (embedded, scores, score_gradient, distill_loss)


MESH = pl.DeviceIdType.MESH
NEG = float("-inf")


def fused_kernel(
    seq_count,
    pb_count,
    lengths_ref,
    groups_ref,
    tokens_ref,
    gain_attn_ref,
    gain_embed_ref,
    queries_ref,
    teacher_ref,
    wk_hbm,
    wv_hbm,
    wq_hbm,
    wo_hbm,
    emb_ref,
    scores_ref,
    grad_ref,
    loss_ref,
    wk,
    wv,
    wq,
    wo,
    kv_send,
    q_send,
    kv,
    q_in,
    m_send,
    m_in,
    query_all,
    a_send,
    a_in,
    own_sum,
    emb,
    sim,
    gmax,
    kl_seq,
    kl_pb,
    w_sem,
    out_sem,
    send,
    recv,
):
    me = lax.axis_index("seq")
    pb = lax.axis_index("pb")
    planes = seq_count // 2
    z, y = me // 2, lax.rem(me, 2)
    core, x = lax.rem(pb, 2), pb // 2
    core_mate = pb + 1 - 2 * core
    x_mate = lax.rem(pb + 2, pb_count)
    y_mate = me + 1 - 2 * y
    rows = tokens_ref.shape[0]
    half = rows // 2
    chunk = half // 2
    own_rows = pl.multiple_of(core * half, half)
    mate_rows = pl.multiple_of((1 - core) * half, half)
    groups = groups_ref.shape[0]

    QU, QD, QY, KZ, KY, TQ, MX, XX = (i * planes for i in range(8))
    CA, CD, WX = 8 * planes, 8 * planes + 1, 8 * planes + 3
    WY = WX + planes - 1
    GM = WY + 1
    LS, LP = GM + seq_count, GM + 2 * seq_count
    VZ = LP + pb_count

    def remote(src, dst, out_place, in_place, where):
        return pltpu.make_async_remote_copy(
            src_ref=src,
            dst_ref=dst,
            send_sem=send.at[out_place],
            recv_sem=recv.at[in_place],
            device_id=where,
            device_id_type=MESH,
        )

    loads = [
        pltpu.make_async_copy(src, dst, w_sem.at[i])
        for i, (src, dst) in enumerate(((wk_hbm, wk), (wv_hbm, wv), (wq_hbm, wq), (wo_hbm, wo.at[x])))
    ]
    for load in loads[:2]:
        load.start()

    barrier = pltpu.get_barrier_semaphore()
    for d in range(1, seq_count):
        pl.semaphore_signal(
            barrier,
            inc=1,
            device_id={"seq": lax.rem(me + d, seq_count)},
            device_id_type=MESH,
        )
    for d in range(1, pb_count):
        pl.semaphore_signal(
            barrier,
            inc=1,
            device_id={"pb": lax.rem(pb + d, pb_count)},
            device_id_type=MESH,
        )
    query_all[me] = queries_ref[0]
    residual = tokens_ref[...].astype(jnp.float32)
    normed = rms_scale(residual, gain_attn_ref[...]).astype(jnp.bfloat16)
    pl.semaphore_wait(barrier, seq_count + pb_count - 2)
    loads[2].start()

    def along(d):
        return lax.rem(z + d, planes)

    sent = []

    def go(copy):
        copy.start()
        sent.append(copy)

    def wanted(i):
        return y * (planes - 1) + (1 - 2 * y) * i

    def fetch(i):
        h = wanted(i)
        return remote(wo_hbm.at[h], wo.at[x, h], WX + i, WX + i, {"pb": x_mate})

    def fetched(i):
        block = wo.at[1 - x, wanted(i)]
        remote(block, block, WX + i, WX + i, {"pb": x_mate}).wait_recv()

    for i in range(planes - 2):
        go(fetch(i))

    def hop(far):
        upward, downward = 2 * (z - far) + y, 2 * (z + far) + y
        up = remote(query_all.at[upward], query_all.at[upward], QU + z - far, QU + z - far, {"seq": me + 2})
        down = remote(query_all.at[downward], query_all.at[downward], QD + z + far, QD + z + far, {"seq": me - 2})
        return ((z >= far) & (z < planes - 1), up), ((z + far < planes) & (z > 0), down)

    def hop_in(far):
        for sign in (-1, 1):
            source = z + sign * far
            slot = 2 * source + y

            @pl.when((source >= 0) & (source < planes))
            def _():
                block = query_all.at[slot]
                place = (QU if sign < 0 else QD) + source
                remote(block, block, place, place, {"seq": me + 2 * sign}).wait_recv()

    def hop_out(far):
        for valid, copy in hop(far):
            pl.when(valid)(copy.start)
        for sign in (-1, 1) if far else (1,):
            source = z + sign * far
            slot = 2 * source + y

            @pl.when((source >= 0) & (source < planes))
            def _():
                block = query_all.at[slot]
                remote(block, block, QY + source, QY + source, {"seq": y_mate}).start()

    hop_out(0)

    loads[0].wait()
    k_all = jnp.dot(normed, wk[...], preferred_element_type=jnp.float32).astype(jnp.bfloat16)
    for h in range(planes):
        kv_send[h, 0] = k_all[:, h * HD : (h + 1) * HD]

    def scatter(which, place):
        for d in range(1, planes):
            other = along(d)
            go(remote(kv_send.at[other, which], kv.at[me, which], place + other, place + z, {"seq": 2 * other + y}))

    scatter(0, KZ)
    loads[3].start()
    loads[1].wait()
    v_all = jnp.dot(normed, wv[...], preferred_element_type=jnp.float32).astype(jnp.bfloat16)
    for h in range(planes):
        kv_send[h, 1] = v_all[:, h * HD : (h + 1) * HD]
    scatter(1, VZ)
    kv[me] = kv_send[z]
    go(remote(kv.at[me], kv.at[me], KY + z, KY + z, {"seq": y_mate}))
    loads[2].wait()
    q_all = jnp.dot(normed, wq[...], preferred_element_type=jnp.float32).astype(jnp.bfloat16)
    for h in range(planes):
        q_send[h] = q_all[:, h * HD : (h + 1) * HD]
    q_in[z] = q_send[z]

    for d in range(1, planes):
        source = along(planes - d)
        slot = 2 * source + y
        for which, place in ((0, KZ), (1, VZ)):
            block = kv.at[slot, which]
            remote(block, block, place + source, place + source, {"seq": slot}).wait_recv()
        go(remote(kv.at[slot], kv.at[slot], KY + source, KY + source, {"seq": y_mate}))
    for d in range(1, planes):
        other = along(d)
        go(remote(q_send.at[other], q_in.at[z], TQ + other, TQ + z, {"seq": 2 * other + y}))
    for d in range(planes):
        source = along(planes - d)
        slot = 2 * source + 1 - y
        remote(kv.at[slot], kv.at[slot], KY + source, KY + source, {"seq": y_mate}).wait_recv()

    span = rows * seq_count
    key_at = lax.broadcasted_iota(jnp.int32, (1, span), 1)
    row_at = lax.broadcasted_iota(jnp.int32, (rows, 1), 0)

    def attend(source):
        query_at = row_at + (2 * source + y) * rows
        seen = (key_at >= query_at - WIN // 2) & (key_at <= query_at + WIN // 2)
        keys = kv[:, 0].reshape(span, HD)
        values = kv[:, 1].reshape(span, HD)
        logits = lax.dot_general(
            q_in[source], keys, (((1,), (1,)), ((), ())), preferred_element_type=jnp.float32
        )
        logits = jnp.where(seen, logits, NEG)
        row_max = jnp.max(logits, axis=-1, keepdims=True)
        terms = jnp.exp2((logits - row_max) * (HD ** (-0.5) / math.log(2.0)))
        total = jnp.sum(terms, axis=-1, keepdims=True)
        out = jnp.dot(terms.astype(jnp.bfloat16), values, preferred_element_type=jnp.float32)
        return (out / total).astype(jnp.bfloat16)

    def over(h):
        return remote(m_in.at[x, h], m_in.at[x, h], XX + h, XX + h, {"pb": x_mate})

    go(fetch(planes - 2))
    fetched(0)
    first = wo.at[1 - x, wanted(0)]
    go(remote(first, first, WY, WY, {"seq": y_mate}))
    hop_in(1)
    hop_out(1)
    m_in[x, z] = attend(z)
    go(over(z))
    for d in range(1, planes):
        source = along(d)
        slot = 2 * source + y
        remote(q_in.at[source], q_in.at[source], TQ + source, TQ + source, {"seq": slot}).wait_recv()
        m_send[source] = attend(source)
        go(remote(m_send.at[source], m_in.at[x, z], MX + source, MX + z, {"seq": slot}))
        if d + 1 < planes:
            hop_in(d + 1)
            hop_out(d + 1)
    for d in range(1, planes):
        source = along(planes - d)
        block = m_in.at[x, source]
        remote(block, block, MX + source, MX + source, {"seq": 2 * source + y}).wait_recv()
        go(over(source))

    loads[3].wait()

    for i in range(1, planes - 1):
        fetched(i)
    last = wo.at[1 - x, wanted(planes - 1)]
    remote(last, last, WY, WY, {"seq": y_mate}).wait_recv()
    for h in range(planes):
        block = m_in.at[1 - x, h]
        remote(block, block, XX + h, XX + h, {"pb": x_mate}).wait_recv()

    def project(first):
        mixed = jnp.concatenate(
            [m_in[i, h, pl.ds(first, half), :] for i in range(2) for h in range(planes)], axis=1
        )
        weight = wo[...].reshape(2 * planes * HD, wo.shape[3])
        return jnp.dot(mixed, weight, preferred_element_type=jnp.float32)

    a_send[...] = project(mate_rows).astype(jnp.bfloat16)
    copy_a = remote(a_send, a_in, CA, CA, {"pb": core_mate})
    go(copy_a)
    own_sum[...] = project(own_rows)
    copy_a.wait_recv()
    for d in range(planes):
        source = along(planes - d)
        slot = 2 * source + 1 - y
        remote(query_all.at[slot], query_all.at[slot], QY + source, QY + source, {"seq": y_mate}).wait_recv()
    for i in range(2):
        here = pl.ds(pl.multiple_of(own_rows + i * chunk, chunk), chunk)
        part = slice(i * chunk, (i + 1) * chunk)
        attn = own_sum[part] + a_in[part].astype(jnp.float32)
        total = tokens_ref[here, :].astype(jnp.float32) + attn
        emb[here, :] = rms_scale(total, gain_embed_ref[...]).astype(jnp.bfloat16)
        go(remote(emb.at[here, :], emb.at[here, :], CD + i, CD + i, {"pb": core_mate}))

    q_rows = query_all[...].reshape(query_all.shape[0] * query_all.shape[1], query_all.shape[2])

    def compare(first):
        sim[pl.ds(first, half), :] = lax.dot_general(
            emb[pl.ds(first, half), :], q_rows, (((1,), (1,)), ((), ())), preferred_element_type=jnp.float32
        )

    compare(own_rows)
    for i in range(2):
        there = pl.ds(pl.multiple_of(mate_rows + i * chunk, chunk), chunk)
        remote(emb.at[there, :], emb.at[there, :], CD + i, CD + i, {"pb": core_mate}).wait_recv()
    store = pltpu.make_async_copy(emb, emb_ref, out_sem)
    store.start()
    compare(mate_rows)

    similar = sim[...]
    position = lax.broadcasted_iota(jnp.int32, similar.shape, 0) + me * rows
    begin = jnp.int32(0)
    for c in range(groups):
        end = begin + groups_ref[c]
        inside = (position >= begin) & (position < end)
        gmax[me, c : c + 1] = jnp.max(jnp.where(inside, similar, NEG), axis=0, keepdims=True)
        begin = end
    for d in range(1, seq_count):
        other = lax.rem(me + d, seq_count)
        go(remote(gmax.at[me], gmax.at[me], GM + other, GM + me, {"seq": other}))
    for d in range(1, seq_count):
        other = lax.rem(me + d, seq_count)
        remote(gmax.at[other], gmax.at[other], GM + other, GM + other, {"seq": other}).wait_recv()
    token_max = jnp.max(gmax[...], axis=0)
    slot_of = lax.broadcasted_iota(jnp.int32, token_max.shape, 1) - me * LQ
    length = lengths_ref[0]
    live = (slot_of >= 0) & (slot_of < length)
    column = jnp.sum(jnp.where(live, token_max, 0.0), axis=1, keepdims=True)
    square = (groups, groups)
    diagonal = lax.broadcasted_iota(jnp.int32, square, 0) == lax.broadcasted_iota(jnp.int32, square, 1)
    row = jnp.sum(jnp.where(diagonal, column, 0.0), axis=0, keepdims=True)
    scores = row / length.astype(jnp.float32)
    scores_ref[...] = scores

    def log_softmax(values):
        values = values / SOFTMAX_TEMP
        values = values - jnp.max(values, axis=-1, keepdims=True)
        return values - jnp.log(jnp.sum(jnp.exp(values), axis=-1, keepdims=True))

    log_s = log_softmax(scores)
    log_t = log_softmax(teacher_ref[...])
    prob = jnp.exp(log_t)
    amount = seq_count * pb_count
    grad_ref[...] = (jnp.exp(log_s) - prob) / (SOFTMAX_TEMP * amount)
    kl = jnp.sum(prob * (log_t - log_s), axis=-1, keepdims=True)
    kl_seq[me] = jnp.broadcast_to(kl, kl_seq.shape[1:])
    for d in range(1, seq_count):
        other = lax.rem(me + d, seq_count)
        go(remote(kl_seq.at[me], kl_seq.at[me], LS + other, LS + me, {"seq": other}))
    for d in range(1, seq_count):
        other = lax.rem(me + d, seq_count)
        remote(kl_seq.at[other], kl_seq.at[other], LS + other, LS + other, {"seq": other}).wait_recv()
    kl_pb[pb] = jnp.sum(kl_seq[...], axis=0)
    for d in range(1, pb_count):
        other = lax.rem(pb + d, pb_count)
        go(remote(kl_pb.at[pb], kl_pb.at[pb], LP + other, LP + pb, {"pb": other}))
    for d in range(1, pb_count):
        other = lax.rem(pb + d, pb_count)
        remote(kl_pb.at[other], kl_pb.at[other], LP + other, LP + other, {"pb": other}).wait_recv()
    loss_ref[...] = jnp.sum(kl_pb[...], axis=0)[:1, :1] / amount

    for copy in sent:
        copy.wait_send()
    for far in range(planes):
        for valid, copy in hop(far):
            pl.when(valid)(copy.wait_send)
    for source in range(planes):
        block = query_all.at[2 * source + y]
        remote(block, block, QY + source, QY + source, {"seq": y_mate}).wait_send()
    store.wait()


def fused(
    tokens,
    w_query,
    w_key,
    w_value,
    w_out,
    gain_attn,
    gain_embed,
    queries,
    query_lengths,
    group_lengths,
    teacher,
):
    seq_count, pb_count = lax.axis_size("seq"), lax.axis_size("pb")
    rows, width = tokens.shape
    head_width = w_query.shape[1]
    planes = seq_count // 2
    groups = group_lengths.shape[0]
    slots = queries.shape[0] * seq_count * LQ
    half = rows // 2
    bf, f32 = jnp.bfloat16, jnp.float32
    vmem, smem = pl.BlockSpec(memory_space=pltpu.VMEM), pl.BlockSpec(memory_space=pltpu.SMEM)
    hbm = pl.BlockSpec(memory_space=pl.ANY)
    copies = 10 * planes + 3 + 2 * seq_count + pb_count
    embedded, scores, grad, loss = pl.pallas_call(
        functools.partial(fused_kernel, seq_count, pb_count),
        out_shape=(
            pltpu.VMEM((rows, width), bf),
            jax.ShapeDtypeStruct((1, groups), f32),
            jax.ShapeDtypeStruct((1, groups), f32),
            jax.ShapeDtypeStruct((1, 1), f32),
        ),
        in_specs=[smem, smem] + [vmem] * 5 + [hbm] * 4,
        out_specs=(vmem, vmem, vmem, vmem),
        scratch_shapes=[
            pltpu.VMEM((width, head_width), bf),
            pltpu.VMEM((width, head_width), bf),
            pltpu.VMEM((width, head_width), bf),
            pltpu.VMEM((2, planes, HD, width), bf),
            pltpu.VMEM((planes, 2, rows, HD), bf),
            pltpu.VMEM((planes, rows, HD), bf),
            pltpu.VMEM((seq_count, 2, rows, HD), bf),
            pltpu.VMEM((planes, rows, HD), bf),
            pltpu.VMEM((planes, rows, HD), bf),
            pltpu.VMEM((2, planes, rows, HD), bf),
            pltpu.VMEM((seq_count, LQ, width), bf),
            pltpu.VMEM((half, width), bf),
            pltpu.VMEM((half, width), bf),
            pltpu.VMEM((half, width), f32),
            pltpu.VMEM((rows, width), bf),
            pltpu.VMEM((rows, slots), f32),
            pltpu.VMEM((seq_count, groups, slots), f32),
            pltpu.VMEM((seq_count, 8, 128), f32),
            pltpu.VMEM((pb_count, 8, 128), f32),
            pltpu.SemaphoreType.DMA((4,)),
            pltpu.SemaphoreType.DMA,
            pltpu.SemaphoreType.DMA((copies,)),
            pltpu.SemaphoreType.DMA((copies,)),
        ],
        compiler_params=pltpu.CompilerParams(
            collective_id=0, has_side_effects=True, vmem_limit_bytes=56 * 1024 * 1024
        ),
    )(
        query_lengths,
        group_lengths,
        tokens,
        gain_attn.reshape(1, width),
        gain_embed.reshape(1, width),
        queries,
        teacher,
        w_key,
        w_value,
        w_query,
        w_out.reshape(planes, HD, width),
    )
    return embedded, scores, grad, loss.reshape(())


def run(*args):
    planes = args[1].shape[1] // HD
    fits = lax.axis_size("seq") == 2 * planes and lax.axis_size("pb") == 4 and args[7].shape[0] == 1
    return fused(*args) if fits else per_device(*args)


def solution(mesh):
    placed = (
        P("seq", None),
        P(None, "pb"),
        P(None, "pb"),
        P(None, "pb"),
        P("pb", None),
        P(),
        P(),
        P(("seq", "pb"), None, None),
        P(("seq", "pb")),
        P(),
        P(("seq", "pb"), None),
    )
    return jax.shard_map(
        run,
        mesh=mesh,
        in_specs=placed,
        out_specs=(P("seq", None), P(("seq", "pb"), None), P(("seq", "pb"), None), P()),
        check_vma=False,
    )
```
